32 devices in a mesh: conf: 2 (over x), tgt: 8 (over z, y), src: 2 (over core).
Axes of the slice: x: 2, y: 2, z: 4, core: 2. Of those that a mesh axis runs over, the one named last changes fastest.
Arguments:
- right_side: float32 [128, 8192], P('conf', ('tgt', 'src')), parts along dimension 0, may hold values from -6 to 6
- atom_centers: float32 [6, 40000], P('conf'), parts along dimension 0, may hold values from -4 to 4
- tessera_owner: int32 [8192], replicated, may hold values from 0 to 39999
- tessera_angles: float32 [2, 8192], replicated, may hold values from -3.140625 to 3.140625
- self_term: float32 [8192], P(('tgt', 'src')), may hold values from 0.5 to 2
Outputs:
- surface_charge: float32 [128, 8192], P('conf', ('tgt', 'src')), parts along dimension 0
- residual: float32 [128, 8192], P('conf', ('tgt', 'src')), parts along dimension 0
The draws below stay inside these ranges and needn't reach their ends.
There are 2 independent parts, one for each index of `conf`. The reference program is written for one: setup_inputs(seed, part) draws one part's arguments, and reference() takes and returns one part's arrays. A program takes and returns all parts, laid end to end along the dimension named above; an argument that names none is the same for every part. Nothing has to cross between parts.
All inputs are finite; a program needn't handle non-finite values.
Results may differ from the reference program's by a relative error of at most 0.006.
The reference program's roundings to bfloat16 on the way count: a program that leaves them out, or rounds other values in their place, can miss the bound.
Values may be sent and summed in bfloat16 or wider, within the bound.
No kernel may reach another device: no remote copies, remote signals or barrier semaphores. Data moves between devices by JAX's collectives and lax.ppermute only.
A program may use at most 128 MiB of HBM per device.

```python
import math
import jax
import jax.numpy as jnp
from jax import lax

K = 64
ATOMS = 40000
ITERS = 2
TESS_DEV = 512
NT = 8192
N_SRC = 2


def plant(array, rng, least, top_value):
    place = [jax.random.randint(jax.random.fold_in(rng, axis), (), 0, length) for axis, length in enumerate(array.shape)]
    widest = array.shape.index(max(array.shape))
    neighbour = place[:widest] + [(place[widest] + 1) % array.shape[widest]] + place[widest + 1:]
    return array.at[tuple(place)].set(least).at[tuple(neighbour)].set(top_value)


def shard_levels(rng, dims, split, low, high):
    def one(axis_at, shards_of):
        steps = jax.random.uniform(jax.random.fold_in(jax.random.fold_in(rng, 6), axis_at), (shards_of,), jnp.float32, low / len(split), high / len(split))
        return jnp.repeat(jnp.exp(steps), dims[axis_at] // shards_of).reshape((-1,) + (1,) * (len(dims) - axis_at - 1))

    gain = one(*split[0])
    for cut in split[1:]:
        gain = gain * one(*cut)
    return gain


def noise(key, shape, scale, bound, shards=(), kind=jnp.bfloat16):
    entries = jax.random.normal(key, shape, jnp.float32) * scale
    if len(shards) > 0:
        entries = shard_levels(key, shape, shards, -0.22, 0.18) * entries
    return jnp.clip(entries, min=-bound, max=bound).astype(kind)


def setup_inputs(seed: int = 0, part: int = 0) -> dict:
    key_of = jax.random.split(jax.random.key(seed), 6)
    own_keys = jax.random.split(jax.random.fold_in(key_of[5], part), 6)
    right_side = noise(own_keys[0], (K, NT), 1.0, 6.0, ((1, 16),), jnp.float32)
    atom_centers = jnp.clip(jax.random.uniform(own_keys[1], (3, ATOMS), jnp.float32, -4.0, 4.0), -4.0, 4.0)
    tessera_owner = plant(jax.random.randint(key_of[2], (NT,), 0, ATOMS), jax.random.fold_in(key_of[2], 1), 0, ATOMS - 1).astype(jnp.int32)
    tessera_angles = jnp.clip(jax.random.uniform(key_of[3], (2, NT), jnp.float32, -3.140625, 3.140625), -3.140625, 3.140625)
    self_term = jnp.clip(jnp.exp(math.log(2.0) - 1.3862944 * jax.random.uniform(key_of[4], (NT,), jnp.float32) ** shard_levels(key_of[4], (NT,), ((0, 16),), -0.2, 0.2)), 0.5, 2.0)
    return {"right_side": right_side, "atom_centers": atom_centers, "tessera_owner": tessera_owner, "tessera_angles": tessera_angles, "self_term": self_term}


soft_square = 0.09
probe_radius = 0.15

def positions(atom_centers, tessera_owner, tessera_angles):
    base = jnp.take(atom_centers, tessera_owner, axis=1)
    azimuth = tessera_angles[0]
    polar = tessera_angles[1]
    sine = jnp.sin(polar)
    offsets = jnp.stack([jnp.cos(azimuth) * sine, jnp.sin(azimuth) * sine, jnp.cos(polar)])
    return base + probe_radius * offsets

def tile_apply(total, source_pos, charges, target_pos):
    diff = source_pos[0][:, None] - target_pos[0][None, :]
    dist_sq = diff * diff
    diff = source_pos[1][:, None] - target_pos[1][None, :]
    dist_sq = dist_sq + diff * diff
    diff = source_pos[2][:, None] - target_pos[2][None, :]
    dist_sq = dist_sq + diff * diff
    kern = lax.rsqrt(dist_sq + soft_square).astype(jnp.bfloat16)
    return total + jnp.dot(charges.astype(jnp.float32), kern.astype(jnp.float32), preferred_element_type=jnp.float32)

def apply_operator(allpos, direction, self_term):
    charges = direction.astype(jnp.bfloat16)
    block = TESS_DEV * N_SRC
    count = NT // block

    def per_target(tindex):
        target_pos = lax.dynamic_slice_in_dim(allpos, tindex * block, block, 1)

        def inner(sindex, total):
            source_pos = lax.dynamic_slice_in_dim(allpos, sindex * block, block, 1)
            piece = lax.dynamic_slice_in_dim(charges, sindex * block, block, 1)
            return tile_apply(total, source_pos, piece, target_pos)
        return lax.fori_loop(0, count, inner, jnp.zeros((direction.shape[0], block), jnp.float32))
    blocks = lax.map(per_target, jnp.arange(count, dtype=jnp.int32))
    near = jnp.transpose(blocks, (1, 0, 2)).reshape(direction.shape[0], NT)
    return near + self_term[None, :] * direction

def products(left, right):
    return lax.dot_general(left.astype(jnp.float32), right.astype(jnp.float32), (((1,), (1,)), ((), ())), precision=lax.Precision.HIGHEST, preferred_element_type=jnp.float32)

def chol_solve(matrix, rhs):
    lower = jnp.linalg.cholesky(matrix)
    middle = lax.linalg.triangular_solve(lower, rhs, left_side=True, lower=True)
    return lax.linalg.triangular_solve(lower, middle, left_side=True, lower=True, transpose_a=True)

def reference(right_side, atom_centers, tessera_owner, tessera_angles, self_term):
    allpos = positions(atom_centers, tessera_owner, tessera_angles)
    solution = jnp.zeros_like(right_side)
    residual = right_side
    direction = right_side
    norm_now = products(residual, residual)
    for step in range(ITERS):
        image = apply_operator(allpos, direction, self_term)
        gram = products(direction, image)
        alpha = chol_solve(gram, norm_now)
        solution = solution + jnp.dot(alpha.T, direction, precision=lax.Precision.HIGHEST)
        residual = residual - jnp.dot(alpha.T, image, precision=lax.Precision.HIGHEST)
        if step + 1 < ITERS:
            norm_next = products(residual, residual)
            beta = chol_solve(norm_now, norm_next)
            direction = residual + jnp.dot(beta.T, direction, precision=lax.Precision.HIGHEST)
            norm_now = norm_next
    return (solution, residual)
```

```python
import functools

import jax
import jax.numpy as jnp
from jax import lax
from jax.experimental import pallas as pl
from jax.experimental.pallas import tpu as pltpu
from jax.sharding import PartitionSpec as P

ITERS = 2
GROUP = 4
LOW = 256
STORED_LIMIT = 32 * 2**20

soft_square = 0.09
probe_radius = 0.15
HIGHEST = lax.Precision.HIGHEST
MIB = 2**20


def params(mib, **kw):
    return pltpu.CompilerParams(vmem_limit_bytes=mib * MIB, **kw)


def positions(atom_centers, tessera_owner, tessera_angles):
    base = jnp.take(atom_centers, tessera_owner, axis=1)
    return base + probe_radius * unit_offsets(tessera_angles)


def unit_offsets(tessera_angles):
    azimuth = tessera_angles[0]
    polar = tessera_angles[1]
    sine = jnp.sin(polar)
    return jnp.stack([jnp.cos(azimuth) * sine, jnp.sin(azimuth) * sine, jnp.cos(polar)])


def tile_apply(total, source_pos, charges, target_pos):
    diff = source_pos[0][:, None] - target_pos[0][None, :]
    dist_sq = diff * diff
    diff = source_pos[1][:, None] - target_pos[1][None, :]
    dist_sq = dist_sq + diff * diff
    diff = source_pos[2][:, None] - target_pos[2][None, :]
    dist_sq = dist_sq + diff * diff
    kern = lax.rsqrt(dist_sq + soft_square).astype(jnp.bfloat16)
    return total + jnp.dot(charges, kern, preferred_element_type=jnp.float32)


def products(left, right):
    return lax.dot_general(
        left,
        right,
        (((1,), (1,)), ((), ())),
        precision=HIGHEST,
        preferred_element_type=jnp.float32,
    )


def chol_solve(matrix, rhs):
    lower = jnp.linalg.cholesky(matrix)
    middle = lax.linalg.triangular_solve(lower, rhs, left_side=True, lower=True)
    return lax.linalg.triangular_solve(lower, middle, left_side=True, lower=True, transpose_a=True)


def per_device_general(right_side, atom_centers, tessera_owner, tessera_angles, self_term):
    shard = right_side.shape[1]
    columns = right_side.shape[0]
    n_src = lax.axis_size("src")
    tgt_index = lax.axis_index("tgt")
    src_index = lax.axis_index("src")
    allpos = positions(atom_centers, tessera_owner, tessera_angles)

    def residual_norm(residual):
        return lax.psum(products(residual, residual), ("tgt", "src"))

    solution = jnp.zeros_like(right_side)
    residual = right_side
    direction = right_side
    norm_now = residual_norm(residual)
    for step in range(ITERS):
        charges = direction.astype(jnp.bfloat16)
        width = shard * n_src
        target_pos = lax.dynamic_slice_in_dim(allpos, tgt_index * width, width, 1)
        empty = jnp.zeros((columns, width), jnp.float32)
        piece = lax.all_gather(charges, "tgt", axis=1, tiled=True)
        sub = min(piece.shape[1], shard)
        count = piece.shape[1] // sub

        def one_block(j, acc):
            column = j * sub
            row_first = column // shard * width + src_index * shard + column % shard
            source_pos = lax.dynamic_slice_in_dim(allpos, row_first, sub, 1)
            part = lax.dynamic_slice_in_dim(piece, j * sub, sub, 1)
            return tile_apply(acc, source_pos, part, target_pos)

        partial_value = lax.fori_loop(0, count, one_block, empty)
        near = lax.psum_scatter(partial_value, "src", scatter_dimension=1, tiled=True)
        image = near + self_term[None, :] * direction
        gram = lax.psum(products(direction, image), ("tgt", "src"))
        alpha = chol_solve(gram, norm_now)
        solution = solution + jnp.dot(alpha.T, direction, precision=HIGHEST)
        residual = residual - jnp.dot(alpha.T, image, precision=HIGHEST)
        if step + 1 < ITERS:
            norm_next = residual_norm(residual)
            beta = chol_solve(norm_now, norm_next)
            direction = residual + jnp.dot(beta.T, direction, precision=HIGHEST)
            norm_now = norm_next
    return (solution, residual)


def three_parts(value):
    first = value.astype(jnp.bfloat16)
    rest = value - first.astype(jnp.float32)
    second = rest.astype(jnp.bfloat16)
    third = (rest - second.astype(jnp.float32)).astype(jnp.bfloat16)
    return first, second, third


def position_kernel(starts, table_ref, owner_ref, offset_ref, out_ref, parts_ref, *, chunk, count, rows):
    for part, value in enumerate(three_parts(table_ref[...])):
        parts_ref[part * 3 * rows : (part + 1) * 3 * rows, :] = value

    def one(j, carry):
        first = pl.multiple_of(starts[j], chunk)
        at = pl.multiple_of(j * chunk, chunk)
        owner = owner_ref[:, pl.ds(first, chunk)]
        low = lax.broadcasted_iota(jnp.int32, (LOW, chunk), 0) == (owner & (LOW - 1))
        rows_of = jnp.dot(parts_ref[...], low.astype(jnp.bfloat16), preferred_element_type=jnp.float32)
        high = lax.broadcasted_iota(jnp.int32, (rows, chunk), 0) == (owner // LOW)
        for axis in range(3):
            value = rows_of[axis * rows : (axis + 1) * rows]
            for part in range(1, 3):
                place = (part * 3 + axis) * rows
                value = value + rows_of[place : place + rows]
            base = jnp.sum(jnp.where(high, value, 0.0), axis=0, keepdims=True)
            out_ref[axis : axis + 1, pl.ds(at, chunk)] = base + probe_radius * offset_ref[axis : axis + 1, pl.ds(first, chunk)]
        return carry

    lax.fori_loop(0, count, one, 0)


def chosen_positions(table, owner, offsets, starts, chunk):
    count = starts.shape[0]
    rows = table.shape[0] // 3
    whole = pl.BlockSpec(memory_space=pltpu.VMEM)
    return pl.pallas_call(
        functools.partial(position_kernel, chunk=chunk, count=count, rows=rows),
        out_shape=jax.ShapeDtypeStruct((3, count * chunk), jnp.float32),
        in_specs=[pl.BlockSpec(memory_space=pltpu.SMEM), whole, whole, whole],
        out_specs=whole,
        scratch_shapes=[pltpu.VMEM((9 * rows, LOW), jnp.bfloat16)],
        compiler_params=params(24),
        cost_estimate=pl.CostEstimate(flops=2 * 9 * rows * LOW * count * chunk, bytes_accessed=4 * 40000 * 3, transcendentals=0),
        name="positions",
    )(starts, table, owner, offsets)


def entry_kernel(source_ref, target_ref, out_ref):
    dist_sq = None
    for axis in range(3):
        diff = source_ref[:, axis : axis + 1] - target_ref[axis : axis + 1, :]
        dist_sq = diff * diff if dist_sq is None else dist_sq + diff * diff
    out_ref[...] = lax.rsqrt(dist_sq + soft_square).astype(jnp.bfloat16)


def entries(source_pos, target_pos):
    n, m = source_pos.shape[0], target_pos.shape[1]
    step = 256
    return pl.pallas_call(
        entry_kernel,
        grid=(n // step,),
        out_shape=jax.ShapeDtypeStruct((n, m), jnp.bfloat16),
        in_specs=[pl.BlockSpec((step, 3), lambda i: (i, 0)), pl.BlockSpec((3, m), lambda i: (0, 0))],
        out_specs=pl.BlockSpec((step, m), lambda i: (i, 0)),
        compiler_params=params(16),
        cost_estimate=pl.CostEstimate(flops=12 * n * m, bytes_accessed=2 * n * m, transcendentals=n * m),
        name="entries",
    )(source_pos, target_pos)


def apply_kernel(*refs, pieces, per):
    charge_refs, kern_ref, out_ref = refs[:pieces], refs[pieces], refs[pieces + 1]
    j = pl.program_id(0)

    @pl.when(j == 0)
    def _():
        out_ref[...] = jnp.zeros_like(out_ref)

    for piece in range(pieces):
        for part in range(per):

            @pl.when(j == piece * per + part)
            def _(piece=piece, part=part):
                step = kern_ref.shape[0]
                charges = charge_refs[piece][:, part * step : (part + 1) * step]
                out_ref[...] += jnp.dot(charges, kern_ref[...], preferred_element_type=jnp.float32)


def apply_entries(charges, kern):
    pieces = len(charges)
    k, n = charges[0].shape
    m = kern.shape[1]
    step = 512
    per = n // step
    return pl.pallas_call(
        functools.partial(apply_kernel, pieces=pieces, per=per),
        grid=(pieces * per,),
        out_shape=jax.ShapeDtypeStruct((k, m), jnp.float32),
        in_specs=[pl.BlockSpec((k, n), lambda j: (0, 0))] * pieces + [pl.BlockSpec((step, m), lambda j: (j, 0))],
        out_specs=pl.BlockSpec((k, m), lambda j: (0, 0)),
        compiler_params=params(24),
        cost_estimate=pl.CostEstimate(flops=2 * k * n * pieces * m, bytes_accessed=2 * pieces * n * m, transcendentals=0),
        name="apply",
    )(*charges, kern)


def dots(left, right):
    return lax.dot_general(left, right, (((1,), (1,)), ((), ())), precision=HIGHEST, preferred_element_type=jnp.float32)


def left_t(left, right):
    return lax.dot_general(left, right, (((0,), (0,)), ((), ())), precision=HIGHEST, preferred_element_type=jnp.float32)


def mul(left, right):
    return jnp.dot(left, right, precision=HIGHEST, preferred_element_type=jnp.float32)


def eliminate(systems):
    k = systems[0].shape[0]
    row_of = lax.broadcasted_iota(jnp.int32, systems[0].shape, 0)
    systems = list(systems)
    for i in range(k):
        for s, system in enumerate(systems):
            row = system[i : i + 1, :] / system[i : i + 1, i : i + 1]
            systems[s] = jnp.where(row_of == i, row, system - system[:, i : i + 1] * row)
    return [system[:, k:] for system in systems]


def fold(square):
    half = square.shape[0] // 2
    return jnp.concatenate([square[:half], square[half:]], axis=1)


def unfold(folded):
    k = folded.shape[1] // 2
    return jnp.concatenate([folded[:, :k], folded[:, k:]], axis=0)


def first_gram_kernel(own_ref, other_ref, self_ref, direction_ref, image_ref, gram_ref):
    direction = direction_ref[...]
    image = own_ref[...] + other_ref[...] + self_ref[...] * direction
    image_ref[...] = image
    k = direction.shape[0]
    both = dots(jnp.concatenate([direction, image], axis=0), image)
    gram_ref[:k, :] = jnp.concatenate([both[:k], both[k:]], axis=1)
    gram_ref[k:, :] = fold(dots(direction, direction))


def first_gram(partial, other, self_row, direction):
    k, n = direction.shape
    mine = pl.BlockSpec((k, n), lambda i: (0, 0))
    whole = pl.BlockSpec(memory_space=pltpu.VMEM)
    return pl.pallas_call(
        first_gram_kernel,
        grid=(1,),
        out_shape=[jax.ShapeDtypeStruct((k, n), jnp.float32), jax.ShapeDtypeStruct((k + k // 2, 2 * k), jnp.float32)],
        in_specs=[mine, whole, whole, whole],
        out_specs=[whole, whole],
        compiler_params=params(16),
        cost_estimate=pl.CostEstimate(flops=6 * 2 * 3 * k * k * n, bytes_accessed=4 * k * n * 4, transcendentals=0),
        name="first_gram",
    )(partial, other, self_row, direction)


def first_update_kernel(*refs, count):
    part_refs, (image_ref, direction_ref, alpha_ref, residual_ref, next_ref, charges_ref) = refs[:count], refs[count:]
    total = sum_of([ref[...] for ref in part_refs])
    k = total.shape[1] // 2
    gram, image_sq, norm = total[:k, :k], total[:k, k:], unfold(total[k:, :])
    norm = 0.5 * (norm + norm.T)
    unit = (lax.broadcasted_iota(jnp.int32, (k, k), 0) == lax.broadcasted_iota(jnp.int32, (k, k), 1)).astype(jnp.float32)
    alpha, inverse = eliminate([
        jnp.concatenate([0.5 * (gram + gram.T), norm], axis=1),
        jnp.concatenate([norm, unit], axis=1),
    ])
    cross = mul(gram, alpha)
    norm_next = norm - cross - cross.T + left_t(alpha, mul(image_sq, alpha))
    beta = mul(inverse, norm_next)
    alpha_ref[:, :k] = alpha
    alpha_ref[:, k:] = norm_next
    direction = direction_ref[...]
    residual = direction - left_t(alpha, image_ref[...])
    residual_ref[...] = residual
    later = residual + left_t(beta, direction)
    next_ref[...] = later
    charges_ref[...] = later.astype(jnp.bfloat16)


def sum_of(values):
    while len(values) > 1:
        values = [values[i] + values[i + 1] for i in range(0, len(values), 2)]
    return values[0]


def first_update(parts, image, direction):
    k, n = direction.shape
    whole = pl.BlockSpec(memory_space=pltpu.VMEM)
    return pl.pallas_call(
        functools.partial(first_update_kernel, count=len(parts)),
        out_shape=[
            jax.ShapeDtypeStruct((k, 2 * k), jnp.float32),
            jax.ShapeDtypeStruct((k, n), jnp.float32),
            jax.ShapeDtypeStruct((k, n), jnp.float32),
            jax.ShapeDtypeStruct((k, n), jnp.bfloat16),
        ],
        in_specs=[whole] * (len(parts) + 2),
        out_specs=[whole] * 4,
        compiler_params=params(16),
        cost_estimate=pl.CostEstimate(flops=6 * 2 * 2 * k * k * n, bytes_accessed=4 * k * n * 5, transcendentals=0),
        name="first_update",
    )(*parts, image, direction)


def second_gram_kernel(own_ref, other_ref, self_ref, direction_ref, image_ref, gram_ref):
    direction = direction_ref[...]
    image = own_ref[...] + other_ref[...] + self_ref[...] * direction
    image_ref[...] = image
    k = direction.shape[0]
    gram_ref[:, :k] = dots(direction, image)
    gram_ref[:, k:] = jnp.zeros((k, k), jnp.float32)


def second_gram(partial, other, self_row, direction):
    k, n = direction.shape
    mine = pl.BlockSpec((k, n), lambda i: (0, 0))
    whole = pl.BlockSpec(memory_space=pltpu.VMEM)
    return pl.pallas_call(
        second_gram_kernel,
        grid=(1,),
        out_shape=[jax.ShapeDtypeStruct((k, n), jnp.float32), jax.ShapeDtypeStruct((k, 2 * k), jnp.float32)],
        in_specs=[mine, whole, whole, whole],
        out_specs=[whole, whole],
        compiler_params=params(16),
        cost_estimate=pl.CostEstimate(flops=6 * 2 * k * k * n, bytes_accessed=4 * k * n * 4, transcendentals=0),
        name="second_gram",
    )(partial, other, self_row, direction)


def last_update_kernel(*refs, count):
    part_refs = refs[:count]
    alpha_ref, first_ref, residual_ref, direction_ref, image_ref, charge_ref, out_ref = refs[count:]
    total = sum_of([ref[...] for ref in part_refs])
    k = total.shape[0]
    gram = total[:, :k]
    (alpha,) = eliminate([jnp.concatenate([0.5 * (gram + gram.T), alpha_ref[:, k:]], axis=1)])
    charge_ref[...] = left_t(alpha_ref[:, :k], first_ref[...]) + left_t(alpha, direction_ref[...])
    out_ref[...] = residual_ref[...] - left_t(alpha, image_ref[...])


def last_update(parts, alpha, first, residual, direction, image):
    k, n = first.shape
    whole = pl.BlockSpec(memory_space=pltpu.VMEM)
    return pl.pallas_call(
        functools.partial(last_update_kernel, count=len(parts)),
        out_shape=[jax.ShapeDtypeStruct((k, n), jnp.float32)] * 2,
        in_specs=[whole] * (len(parts) + 5),
        out_specs=[whole] * 2,
        compiler_params=params(16),
        cost_estimate=pl.CostEstimate(flops=6 * 3 * 2 * k * k * n, bytes_accessed=4 * k * n * 6, transcendentals=0),
        name="last_update",
    )(*parts, alpha, first, residual, direction, image)


def per_device_grouped(right_side, atom_centers, tessera_owner, tessera_angles, self_term):
    columns, shard = right_side.shape
    n_tgt = lax.axis_size("tgt")
    n_src = lax.axis_size("src")
    t = lax.axis_index("tgt")
    s = lax.axis_index("src")
    copies = n_tgt // GROUP
    member = t % GROUP
    ours = t // GROUP
    width = shard * n_src

    def swap(value, bits):
        return lax.ppermute(value, "tgt", [(i, i ^ bits) for i in range(n_tgt)])

    def swap_core(value):
        return lax.ppermute(value, "src", [(0, 1), (1, 0)])

    near = jnp.concatenate([right_side, jnp.broadcast_to(self_term[None, :], (8, shard))], axis=0)
    far = swap(near, GROUP)
    both = jnp.where(ours == 0, jnp.concatenate([near, far], axis=1), jnp.concatenate([far, near], axis=1))
    direction, self_row = both[:columns], both[columns : columns + 1]
    charges = direction.astype(jnp.bfloat16)
    gathered = [charges] + [swap(charges, bits) for bits in range(1, GROUP)]

    table = jnp.pad(atom_centers, ((0, 0), (0, -atom_centers.shape[1] % (LOW * 8)))).reshape(-1, LOW)
    offsets = unit_offsets(tessera_angles.reshape(2, -1, 128)).reshape(3, -1)
    starts = [((member ^ bits) + GROUP * c) * width + s * shard for bits in range(GROUP) for c in range(copies)]
    starts += [(member + GROUP * c) * width + (1 - s) * shard for c in range(copies)]
    pos = chosen_positions(table, tessera_owner[None, :], offsets, jnp.stack(starts).astype(jnp.int32), shard)
    n_near = copies * shard
    n_all = GROUP * n_near
    target_pos = jnp.concatenate([pos[:, :n_near], pos[:, n_all:]], axis=1)
    kern = entries(pos[:, :n_all].T, target_pos)

    def group_sum_parts(value):
        value = value + swap_core(value)
        return [value] + [swap(value, bits) for bits in range(1, GROUP)]

    partial = apply_entries(gathered, kern)
    image, gram = first_gram(partial, swap_core(partial[:, n_near:]), self_row, direction)
    alpha, residual, later, charges = first_update(group_sum_parts(gram), image, direction)

    gathered = [charges] + [swap(charges, bits) for bits in range(1, GROUP)]
    partial = apply_entries(gathered, kern)
    image, gram = second_gram(partial, swap_core(partial[:, n_near:]), self_row, later)
    parts = group_sum_parts(gram)

    def mine(value):
        return lax.dynamic_slice_in_dim(value, ours * shard, shard, 1)

    return tuple(last_update(parts, alpha, right_side, mine(residual), mine(later), mine(image)))


def solution(mesh):
    n_tgt, n_src = mesh.shape["tgt"], mesh.shape["src"]

    def run(right_side, atom_centers, tessera_owner, tessera_angles, self_term):
        total = right_side.shape[1]
        stored = 2 * (total // n_src) * (total // GROUP)
        grouped = n_tgt == 2 * GROUP and n_src == 2 and stored <= STORED_LIMIT
        return jax.shard_map(
            per_device_grouped if grouped else per_device_general,
            mesh=mesh,
            in_specs=(P("conf", ("tgt", "src")), P("conf", None), P(), P(), P(("tgt", "src"))),
            out_specs=(P("conf", ("tgt", "src")), P("conf", ("tgt", "src"))),
            check_vma=False,
        )(right_side, atom_centers, tessera_owner, tessera_angles, self_term)

    return run
```

```python
import functools

import jax
import jax.numpy as jnp
from jax import lax
from jax.experimental import pallas as pl
from jax.experimental.pallas import tpu as pltpu
from jax.sharding import PartitionSpec as P

ITERS = 2
GROUP = 4
LOW = 256
FEATURES = 48
STORED_LIMIT = 32 * 2**20

soft_square = 0.09
probe_radius = 0.15
HIGHEST = lax.Precision.HIGHEST
MIB = 2**20


def params(mib, **kw):
    return pltpu.CompilerParams(vmem_limit_bytes=mib * MIB, **kw)


def positions(atom_centers, tessera_owner, tessera_angles):
    base = jnp.take(atom_centers, tessera_owner, axis=1)
    return base + probe_radius * unit_offsets(tessera_angles)


def unit_offsets(tessera_angles):
    azimuth = tessera_angles[0]
    polar = tessera_angles[1]
    sine = jnp.sin(polar)
    return jnp.stack([jnp.cos(azimuth) * sine, jnp.sin(azimuth) * sine, jnp.cos(polar)])


def tile_apply(total, source_pos, charges, target_pos):
    diff = source_pos[0][:, None] - target_pos[0][None, :]
    dist_sq = diff * diff
    diff = source_pos[1][:, None] - target_pos[1][None, :]
    dist_sq = dist_sq + diff * diff
    diff = source_pos[2][:, None] - target_pos[2][None, :]
    dist_sq = dist_sq + diff * diff
    kern = lax.rsqrt(dist_sq + soft_square).astype(jnp.bfloat16)
    return total + jnp.dot(charges, kern, preferred_element_type=jnp.float32)


def products(left, right):
    return lax.dot_general(
        left,
        right,
        (((1,), (1,)), ((), ())),
        precision=HIGHEST,
        preferred_element_type=jnp.float32,
    )


def chol_solve(matrix, rhs):
    lower = jnp.linalg.cholesky(matrix)
    middle = lax.linalg.triangular_solve(lower, rhs, left_side=True, lower=True)
    return lax.linalg.triangular_solve(lower, middle, left_side=True, lower=True, transpose_a=True)


def per_device_general(right_side, atom_centers, tessera_owner, tessera_angles, self_term):
    shard = right_side.shape[1]
    columns = right_side.shape[0]
    n_src = lax.axis_size("src")
    tgt_index = lax.axis_index("tgt")
    src_index = lax.axis_index("src")
    allpos = positions(atom_centers, tessera_owner, tessera_angles)

    def residual_norm(residual):
        return lax.psum(products(residual, residual), ("tgt", "src"))

    solution = jnp.zeros_like(right_side)
    residual = right_side
    direction = right_side
    norm_now = residual_norm(residual)
    for step in range(ITERS):
        charges = direction.astype(jnp.bfloat16)
        width = shard * n_src
        target_pos = lax.dynamic_slice_in_dim(allpos, tgt_index * width, width, 1)
        empty = jnp.zeros((columns, width), jnp.float32)
        piece = lax.all_gather(charges, "tgt", axis=1, tiled=True)
        sub = min(piece.shape[1], shard)
        count = piece.shape[1] // sub

        def one_block(j, acc):
            column = j * sub
            row_first = column // shard * width + src_index * shard + column % shard
            source_pos = lax.dynamic_slice_in_dim(allpos, row_first, sub, 1)
            part = lax.dynamic_slice_in_dim(piece, j * sub, sub, 1)
            return tile_apply(acc, source_pos, part, target_pos)

        partial_value = lax.fori_loop(0, count, one_block, empty)
        near = lax.psum_scatter(partial_value, "src", scatter_dimension=1, tiled=True)
        image = near + self_term[None, :] * direction
        gram = lax.psum(products(direction, image), ("tgt", "src"))
        alpha = chol_solve(gram, norm_now)
        solution = solution + jnp.dot(alpha.T, direction, precision=HIGHEST)
        residual = residual - jnp.dot(alpha.T, image, precision=HIGHEST)
        if step + 1 < ITERS:
            norm_next = residual_norm(residual)
            beta = chol_solve(norm_now, norm_next)
            direction = residual + jnp.dot(beta.T, direction, precision=HIGHEST)
            norm_now = norm_next
    return (solution, residual)


def three_parts(value):
    first = value.astype(jnp.bfloat16)
    rest = value - first.astype(jnp.float32)
    second = rest.astype(jnp.bfloat16)
    third = (rest - second.astype(jnp.float32)).astype(jnp.bfloat16)
    return first, second, third


def position_kernel(starts, table_ref, owner_ref, offset_ref, out_ref, parts_ref, *, chunk, count, rows):
    for part, value in enumerate(three_parts(table_ref[...])):
        parts_ref[:, part * LOW : (part + 1) * LOW] = value

    def one(j, carry):
        first = pl.multiple_of(starts[j], chunk)
        at = pl.multiple_of(j * chunk, chunk)
        owner = owner_ref[:, pl.ds(first, chunk)]
        low = lax.broadcasted_iota(jnp.int32, (LOW, chunk), 0) == (owner & (LOW - 1))
        low = low.astype(jnp.bfloat16)
        rows_of = jnp.dot(parts_ref[...], jnp.concatenate([low] * 3, axis=0), preferred_element_type=jnp.float32)
        high = lax.broadcasted_iota(jnp.int32, (rows, chunk), 0) == (owner // LOW)
        for axis in range(3):
            base = jnp.sum(jnp.where(high, rows_of[axis * rows : (axis + 1) * rows], 0.0), axis=0, keepdims=True)
            out_ref[axis : axis + 1, pl.ds(at, chunk)] = base + probe_radius * offset_ref[axis : axis + 1, pl.ds(first, chunk)]
        return carry

    lax.fori_loop(0, count, one, 0)


def chosen_positions(table, owner, offsets, starts, chunk):
    count = starts.shape[0]
    rows = table.shape[0] // 3
    whole = pl.BlockSpec(memory_space=pltpu.VMEM)
    return pl.pallas_call(
        functools.partial(position_kernel, chunk=chunk, count=count, rows=rows),
        out_shape=jax.ShapeDtypeStruct((3, count * chunk), jnp.float32),
        in_specs=[pl.BlockSpec(memory_space=pltpu.SMEM), whole, whole, whole],
        out_specs=whole,
        scratch_shapes=[pltpu.VMEM((3 * rows, 3 * LOW), jnp.bfloat16)],
        compiler_params=params(24),
        cost_estimate=pl.CostEstimate(flops=2 * 9 * rows * LOW * count * chunk, bytes_accessed=4 * 40000 * 3, transcendentals=0),
        name="positions",
    )(starts, table, owner, offsets)


def features(pos, source):
    axes = [pos[axis : axis + 1] for axis in range(3)]
    square = axes[0] * axes[0] + axes[1] * axes[1] + axes[2] * axes[2]
    one = jnp.ones_like(square).astype(jnp.bfloat16)
    rows = []
    for value in axes:
        parts = three_parts(-2.0 * value if source else value)
        pairs = [(0, 0), (0, 1), (1, 0), (0, 2), (1, 1), (2, 0), (1, 2), (2, 1), (2, 2)]
        rows += [parts[pair[0] if source else pair[1]] for pair in pairs]
    if source:
        rows += [*three_parts(square), one, one, one]
    else:
        rows += [one, one, one, *three_parts(square + soft_square)]
    rows += [jnp.zeros_like(one)] * (FEATURES - len(rows))
    return jnp.concatenate(rows, axis=0)


def entry_kernel(source_ref, target_ref, *refs):
    out_refs, (source_rows, target_cols) = refs[:-2], refs[-2:]
    n = source_ref.shape[1]
    source_rows[...] = features(source_ref[...], True).T
    target_cols[...] = features(target_ref[...], False)
    n_out, m = out_refs[0].shape
    step, wide = 512, min(m, 1024)
    for piece, out_ref in enumerate(out_refs):

        def one(i, carry, piece=piece, out_ref=out_ref):
            at = pl.multiple_of(i * step, step)
            rows = source_rows[pl.ds(piece * n_out + at, step), :]
            for j in range(0, m, wide):
                dist_sq = jnp.dot(rows, target_cols[:, j : j + wide], preferred_element_type=jnp.float32)
                out_ref[pl.ds(at, step), j : j + wide] = lax.rsqrt(dist_sq).astype(jnp.bfloat16)
            return carry

        lax.fori_loop(0, n_out // step, one, 0)


def entries(source_pos, target_pos, pieces):
    n, m = source_pos.shape[1], target_pos.shape[1]
    whole = pl.BlockSpec(memory_space=pltpu.VMEM)
    return pl.pallas_call(
        entry_kernel,
        out_shape=[jax.ShapeDtypeStruct((n // pieces, m), jnp.bfloat16)] * pieces,
        in_specs=[whole, whole],
        out_specs=[whole] * pieces,
        scratch_shapes=[pltpu.VMEM((n, FEATURES), jnp.bfloat16), pltpu.VMEM((FEATURES, m), jnp.bfloat16)],
        compiler_params=params(32),
        cost_estimate=pl.CostEstimate(flops=12 * n * m, bytes_accessed=2 * n * m, transcendentals=n * m),
        name="entries",
    )(source_pos, target_pos)


def apply_kernel(*refs, pieces, more):
    charge_refs, kern_refs, out_ref = refs[:pieces], refs[pieces : 2 * pieces], refs[-1]
    wide = 512
    for j in range(0, out_ref.shape[1], wide):
        total = refs[2 * pieces][:, j : j + wide] if more else None
        for charge_ref, kern_ref in zip(charge_refs, kern_refs):
            part = jnp.dot(charge_ref[...], kern_ref[:, j : j + wide], preferred_element_type=jnp.float32)
            total = part if total is None else total + part
        out_ref[:, j : j + wide] = total


def apply_entries(charges, kerns, total=None):
    pieces = len(charges)
    k, n = charges[0].shape
    m = kerns[0].shape[1]
    whole = pl.BlockSpec(memory_space=pltpu.VMEM)
    more = [] if total is None else [total]
    return pl.pallas_call(
        functools.partial(apply_kernel, pieces=pieces, more=bool(more)),
        out_shape=jax.ShapeDtypeStruct((k, m), jnp.float32),
        in_specs=[whole] * (2 * pieces + len(more)),
        out_specs=whole,
        compiler_params=params(32),
        cost_estimate=pl.CostEstimate(flops=8 * k * n * pieces * m, bytes_accessed=2 * pieces * n * m, transcendentals=0),
        name="apply",
    )(*charges, *kerns, *more)


def dots(left, right):
    return lax.dot_general(left, right, (((1,), (1,)), ((), ())), precision=HIGHEST, preferred_element_type=jnp.float32)


def left_t(left, right):
    return lax.dot_general(left, right, (((0,), (0,)), ((), ())), precision=HIGHEST, preferred_element_type=jnp.float32)


def mul(left, right):
    return jnp.dot(left, right, precision=HIGHEST, preferred_element_type=jnp.float32)


def inverse_of_pair(a, b, c):
    scale = 1.0 / (a * c - b * b)
    return c * scale, -b * scale, a * scale


def eliminate_four(system, i, row_of):
    col = [jnp.broadcast_to(system[:, i + j : i + j + 1], system.shape) for j in range(4)]
    row = [system[i + j : i + j + 1, :] for j in range(4)]

    def entry(r, c):
        return col[c][i + r : i + r + 1]

    a, b, d = inverse_of_pair(entry(0, 0), entry(1, 0), entry(1, 1))
    t0, t1 = a * row[0] + b * row[1], b * row[0] + d * row[1]
    b00, b01, b10, b11 = entry(2, 0), entry(3, 0), entry(2, 1), entry(3, 1)
    e00, e10 = a * b00 + b * b10, b * b00 + d * b10
    e01, e11 = a * b01 + b * b11, b * b01 + d * b11
    u, v, w = inverse_of_pair(
        entry(2, 2) - (b00 * e00 + b10 * e10),
        entry(3, 2) - (b00 * e01 + b10 * e11),
        entry(3, 3) - (b01 * e01 + b11 * e11),
    )
    y0, y1 = row[2] - (b00 * t0 + b10 * t1), row[3] - (b01 * t0 + b11 * t1)
    q2, q3 = u * y0 + v * y1, v * y0 + w * y1
    solved = [t0 - (e00 * q2 + e01 * q3), t1 - (e10 * q2 + e11 * q3), q2, q3]
    rest = (system - (col[0] * solved[0] + col[1] * solved[1])) - (col[2] * solved[2] + col[3] * solved[3])
    for j in range(4):
        rest = jnp.where(row_of == i + j, solved[j], rest)
    return rest


def eliminate(systems):
    k = systems[0].shape[0]
    row_of = lax.broadcasted_iota(jnp.int32, systems[0].shape, 0)
    for i in range(0, k, 4):
        systems = [eliminate_four(system, i, row_of) for system in systems]
    return [system[:, k:] for system in systems]


def fold(square):
    half = square.shape[0] // 2
    return jnp.concatenate([square[:half], square[half:]], axis=1)


def unfold(folded):
    k = folded.shape[1] // 2
    return jnp.concatenate([folded[:, :k], folded[:, k:]], axis=0)


def first_gram_kernel(own_ref, other_ref, self_ref, direction_ref, image_ref, gram_ref):
    direction = direction_ref[...]
    image = own_ref[...] + other_ref[...] + self_ref[...] * direction
    image_ref[...] = image
    k = direction.shape[0]
    both = dots(jnp.concatenate([direction, image], axis=0), image)
    gram_ref[:k, :] = jnp.concatenate([both[:k], both[k:]], axis=1)
    gram_ref[k:, :] = fold(dots(direction, direction))


def first_gram(partial, other, self_row, direction):
    k, n = direction.shape
    mine = pl.BlockSpec((k, n), lambda i: (0, 0))
    whole = pl.BlockSpec(memory_space=pltpu.VMEM)
    return pl.pallas_call(
        first_gram_kernel,
        grid=(1,),
        out_shape=[jax.ShapeDtypeStruct((k, n), jnp.float32), jax.ShapeDtypeStruct((k + k // 2, 2 * k), jnp.float32)],
        in_specs=[mine, whole, whole, whole],
        out_specs=[whole, whole],
        compiler_params=params(16),
        cost_estimate=pl.CostEstimate(flops=6 * 2 * 3 * k * k * n, bytes_accessed=4 * k * n * 4, transcendentals=0),
        name="first_gram",
    )(partial, other, self_row, direction)


def first_update_kernel(*refs, count):
    part_refs, (image_ref, direction_ref, alpha_ref, next_ref, charges_ref) = refs[:count], refs[count:]
    total = sum_of([ref[...] for ref in part_refs])
    k = total.shape[1] // 2
    gram, image_sq, norm = total[:k, :k], total[:k, k:], unfold(total[k:, :])
    norm = 0.5 * (norm + norm.T)
    unit = (lax.broadcasted_iota(jnp.int32, (k, k), 0) == lax.broadcasted_iota(jnp.int32, (k, k), 1)).astype(jnp.float32)
    alpha, inverse = eliminate([
        jnp.concatenate([0.5 * (gram + gram.T), norm], axis=1),
        jnp.concatenate([norm, unit], axis=1),
    ])
    both = mul(jnp.concatenate([gram, image_sq], axis=0), alpha)
    cross = both[:k]
    norm_next = norm - cross - cross.T + left_t(alpha, both[k:])
    beta = mul(inverse, norm_next)
    alpha_ref[:, :k] = alpha
    alpha_ref[:, k:] = norm_next
    direction = direction_ref[...]
    weights = jnp.concatenate([beta, -alpha], axis=0)
    later = direction + left_t(weights, jnp.concatenate([direction, image_ref[...]], axis=0))
    next_ref[...] = later
    charges_ref[...] = later.astype(jnp.bfloat16)


def sum_of(values):
    while len(values) > 1:
        values = [values[i] + values[i + 1] for i in range(0, len(values), 2)]
    return values[0]


def first_update(parts, image, direction):
    k, n = direction.shape
    whole = pl.BlockSpec(memory_space=pltpu.VMEM)
    return pl.pallas_call(
        functools.partial(first_update_kernel, count=len(parts)),
        out_shape=[
            jax.ShapeDtypeStruct((k, 2 * k), jnp.float32),
            jax.ShapeDtypeStruct((k, n), jnp.float32),
            jax.ShapeDtypeStruct((k, n), jnp.bfloat16),
        ],
        in_specs=[whole] * (len(parts) + 2),
        out_specs=[whole] * 3,
        compiler_params=params(16),
        cost_estimate=pl.CostEstimate(flops=6 * 2 * 2 * k * k * n, bytes_accessed=4 * k * n * 5, transcendentals=0),
        name="first_update",
    )(*parts, image, direction)


def second_gram_kernel(own_ref, other_ref, self_ref, direction_ref, image_ref, gram_ref):
    direction = direction_ref[...]
    image = own_ref[...] + other_ref[...] + self_ref[...] * direction
    image_ref[...] = image
    k = direction.shape[0]
    gram_ref[:, :k] = dots(direction, image)
    gram_ref[:, k:] = jnp.zeros((k, k), jnp.float32)


def second_gram(partial, other, self_row, direction):
    k, n = direction.shape
    mine = pl.BlockSpec((k, n), lambda i: (0, 0))
    whole = pl.BlockSpec(memory_space=pltpu.VMEM)
    return pl.pallas_call(
        second_gram_kernel,
        grid=(1,),
        out_shape=[jax.ShapeDtypeStruct((k, n), jnp.float32), jax.ShapeDtypeStruct((k, 2 * k), jnp.float32)],
        in_specs=[mine, whole, whole, whole],
        out_specs=[whole, whole],
        compiler_params=params(16),
        cost_estimate=pl.CostEstimate(flops=6 * 2 * k * k * n, bytes_accessed=4 * k * n * 4, transcendentals=0),
        name="second_gram",
    )(partial, other, self_row, direction)


def first_state_kernel(alpha_ref, direction_ref, image_ref, out_ref):
    k, n = direction_ref.shape
    alpha = alpha_ref[:, :k]
    both = left_t(alpha, jnp.concatenate([direction_ref[...], image_ref[...]], axis=1))
    out_ref[:, :n] = both[:, :n]
    out_ref[:, n:] = direction_ref[...] - both[:, n:]


def first_state(alpha, direction, image):
    k, n = direction.shape
    whole = pl.BlockSpec(memory_space=pltpu.VMEM)
    return pl.pallas_call(
        first_state_kernel,
        out_shape=jax.ShapeDtypeStruct((k, 2 * n), jnp.float32),
        in_specs=[whole] * 3,
        out_specs=whole,
        compiler_params=params(16),
        cost_estimate=pl.CostEstimate(flops=6 * 2 * 2 * k * k * n, bytes_accessed=4 * k * n * 4, transcendentals=0),
        name="first_state",
    )(alpha, direction, image)


def last_update_kernel(*refs, count):
    part_refs = refs[:count]
    alpha_ref, state_ref, direction_ref, image_ref, charge_ref, out_ref = refs[count:]
    total = sum_of([ref[...] for ref in part_refs])
    k = total.shape[0]
    n = direction_ref.shape[1]
    gram = total[:, :k]
    (alpha,) = eliminate([jnp.concatenate([0.5 * (gram + gram.T), alpha_ref[:, k:]], axis=1)])
    both = left_t(alpha, jnp.concatenate([direction_ref[...], image_ref[...]], axis=1))
    charge_ref[...] = state_ref[:, :n] + both[:, :n]
    out_ref[...] = state_ref[:, n:] - both[:, n:]


def last_update(parts, alpha, state, direction, image):
    k, n = direction.shape
    whole = pl.BlockSpec(memory_space=pltpu.VMEM)
    return pl.pallas_call(
        functools.partial(last_update_kernel, count=len(parts)),
        out_shape=[jax.ShapeDtypeStruct((k, n), jnp.float32)] * 2,
        in_specs=[whole] * (len(parts) + 4),
        out_specs=[whole] * 2,
        compiler_params=params(16),
        cost_estimate=pl.CostEstimate(flops=6 * 3 * 2 * k * k * n, bytes_accessed=4 * k * n * 6, transcendentals=0),
        name="last_update",
    )(*parts, alpha, state, direction, image)


def per_device_grouped(right_side, atom_centers, tessera_owner, tessera_angles, self_term):
    columns, shard = right_side.shape
    n_tgt = lax.axis_size("tgt")
    n_src = lax.axis_size("src")
    t = lax.axis_index("tgt")
    s = lax.axis_index("src")
    copies = n_tgt // GROUP
    member = t % GROUP
    ours = t // GROUP
    width = shard * n_src

    def swap(value, bits):
        return lax.ppermute(value, "tgt", [(i, i ^ bits) for i in range(n_tgt)])

    def swap_core(value):
        return lax.ppermute(value, "src", [(0, 1), (1, 0)])

    near = jnp.concatenate([right_side, self_term[None, :]], axis=0)
    far = swap(near, GROUP)
    both = jnp.where(ours == 0, jnp.concatenate([near, far], axis=1), jnp.concatenate([far, near], axis=1))
    direction, self_row = both[:columns], both[columns : columns + 1]
    charges = direction.astype(jnp.bfloat16)
    gathered = [charges] + [swap(charges, bits) for bits in range(1, GROUP)]

    table = jnp.pad(atom_centers, ((0, 0), (0, -atom_centers.shape[1] % (LOW * 8)))).reshape(-1, LOW)
    angles = lax.optimization_barrier(tessera_angles.reshape(2, -1, 128))
    offsets = lax.optimization_barrier(unit_offsets(angles)).reshape(3, -1)
    starts = [((member ^ bits) + GROUP * c) * width + s * shard for bits in range(GROUP) for c in range(copies)]
    starts += [(member + GROUP * c) * width + (1 - s) * shard for c in range(copies)]
    pos = chosen_positions(table, tessera_owner[None, :], offsets, jnp.stack(starts).astype(jnp.int32), shard)
    n_near = copies * shard
    n_all = GROUP * n_near
    target_pos = jnp.concatenate([pos[:, :n_near], pos[:, n_all:]], axis=1)
    kerns = entries(pos[:, :n_all], target_pos, GROUP)

    def group_sum_parts(value):
        value = value + swap_core(value)
        return [value] + [swap(value, bits) for bits in range(1, GROUP)]

    def mine(value):
        return lax.dynamic_slice_in_dim(value, ours * shard, shard, 1)

    partial = apply_entries(gathered, kerns)
    image, gram = first_gram(partial, swap_core(partial[:, n_near:]), self_row, direction)
    alpha, later, charges = first_update(group_sum_parts(gram), image, direction)

    gathered = [swap(charges, bits) for bits in range(1, GROUP)]
    partial = apply_entries([charges], kerns[:1])
    for piece, kern in zip(gathered, kerns[1:]):
        partial = apply_entries([piece], [kern], partial)
    state = first_state(alpha, right_side, mine(image))
    image, gram = second_gram(partial, swap_core(partial[:, n_near:]), self_row, later)
    return tuple(last_update(group_sum_parts(gram), alpha, state, mine(later), mine(image)))


def solution(mesh):
    n_tgt, n_src = mesh.shape["tgt"], mesh.shape["src"]

    def run(right_side, atom_centers, tessera_owner, tessera_angles, self_term):
        total = right_side.shape[1]
        stored = 2 * (total // n_src) * (total // GROUP)
        grouped = n_tgt == 2 * GROUP and n_src == 2 and stored <= STORED_LIMIT
        return jax.shard_map(
            per_device_grouped if grouped else per_device_general,
            mesh=mesh,
            in_specs=(P("conf", ("tgt", "src")), P("conf", None), P(), P(), P(("tgt", "src"))),
            out_specs=(P("conf", ("tgt", "src")), P("conf", ("tgt", "src"))),
            check_vma=False,
        )(right_side, atom_centers, tessera_owner, tessera_angles, self_term)

    return run
```

```python
import functools

import jax
import jax.numpy as jnp
from jax import lax
from jax.experimental import pallas as pl
from jax.experimental.pallas import tpu as pltpu
from jax.sharding import PartitionSpec as P

ITERS = 2
GROUP = 4
LOW = 256
FEATURES = 48
UNROLL = 2
STORED_LIMIT = 32 * 2**20

soft_square = 0.09
probe_radius = 0.15
HIGHEST = lax.Precision.HIGHEST
MIB = 2**20


def params(mib, **kw):
    return pltpu.CompilerParams(vmem_limit_bytes=mib * MIB, **kw)


def positions(atom_centers, tessera_owner, tessera_angles):
    base = jnp.take(atom_centers, tessera_owner, axis=1)
    return base + probe_radius * unit_offsets(tessera_angles)


def unit_offsets(tessera_angles):
    azimuth = tessera_angles[0]
    polar = tessera_angles[1]
    sine = jnp.sin(polar)
    return jnp.stack([jnp.cos(azimuth) * sine, jnp.sin(azimuth) * sine, jnp.cos(polar)])


def tile_apply(total, source_pos, charges, target_pos):
    diff = source_pos[0][:, None] - target_pos[0][None, :]
    dist_sq = diff * diff
    diff = source_pos[1][:, None] - target_pos[1][None, :]
    dist_sq = dist_sq + diff * diff
    diff = source_pos[2][:, None] - target_pos[2][None, :]
    dist_sq = dist_sq + diff * diff
    kern = lax.rsqrt(dist_sq + soft_square).astype(jnp.bfloat16)
    return total + jnp.dot(charges, kern, preferred_element_type=jnp.float32)


def products(left, right):
    return lax.dot_general(
        left,
        right,
        (((1,), (1,)), ((), ())),
        precision=HIGHEST,
        preferred_element_type=jnp.float32,
    )


def chol_solve(matrix, rhs):
    lower = jnp.linalg.cholesky(matrix)
    middle = lax.linalg.triangular_solve(lower, rhs, left_side=True, lower=True)
    return lax.linalg.triangular_solve(lower, middle, left_side=True, lower=True, transpose_a=True)


def per_device_general(right_side, atom_centers, tessera_owner, tessera_angles, self_term):
    shard = right_side.shape[1]
    columns = right_side.shape[0]
    n_src = lax.axis_size("src")
    tgt_index = lax.axis_index("tgt")
    src_index = lax.axis_index("src")
    allpos = positions(atom_centers, tessera_owner, tessera_angles)

    def residual_norm(residual):
        return lax.psum(products(residual, residual), ("tgt", "src"))

    solution = jnp.zeros_like(right_side)
    residual = right_side
    direction = right_side
    norm_now = residual_norm(residual)
    for step in range(ITERS):
        charges = direction.astype(jnp.bfloat16)
        width = shard * n_src
        target_pos = lax.dynamic_slice_in_dim(allpos, tgt_index * width, width, 1)
        empty = jnp.zeros((columns, width), jnp.float32)
        piece = lax.all_gather(charges, "tgt", axis=1, tiled=True)
        sub = min(piece.shape[1], shard)
        count = piece.shape[1] // sub

        def one_block(j, acc):
            column = j * sub
            row_first = column // shard * width + src_index * shard + column % shard
            source_pos = lax.dynamic_slice_in_dim(allpos, row_first, sub, 1)
            part = lax.dynamic_slice_in_dim(piece, j * sub, sub, 1)
            return tile_apply(acc, source_pos, part, target_pos)

        partial_value = lax.fori_loop(0, count, one_block, empty)
        near = lax.psum_scatter(partial_value, "src", scatter_dimension=1, tiled=True)
        image = near + self_term[None, :] * direction
        gram = lax.psum(products(direction, image), ("tgt", "src"))
        alpha = chol_solve(gram, norm_now)
        solution = solution + jnp.dot(alpha.T, direction, precision=HIGHEST)
        residual = residual - jnp.dot(alpha.T, image, precision=HIGHEST)
        if step + 1 < ITERS:
            norm_next = residual_norm(residual)
            beta = chol_solve(norm_now, norm_next)
            direction = residual + jnp.dot(beta.T, direction, precision=HIGHEST)
            norm_now = norm_next
    return (solution, residual)


def three_parts(value):
    first = value.astype(jnp.bfloat16)
    rest = value - first.astype(jnp.float32)
    second = rest.astype(jnp.bfloat16)
    third = (rest - second.astype(jnp.float32)).astype(jnp.bfloat16)
    return first, second, third


def position_kernel(starts, table_ref, tail_ref, owner_ref, offset_ref, out_ref, parts_ref, *, chunk, count, rows):
    full = table_ref.shape[0] // 3
    tail = tail_ref.shape[1]
    for axis in range(3):
        first = axis * rows
        if full < rows:
            parts_ref[first + full // 8 * 8 : first + rows, :] = jnp.zeros((rows - full // 8 * 8, 3 * LOW), jnp.bfloat16)
        for part, value in enumerate(three_parts(table_ref[axis * full : (axis + 1) * full])):
            parts_ref[first : first + full, part * LOW : (part + 1) * LOW] = value
        for part, value in enumerate(three_parts(tail_ref[axis : axis + 1])):
            parts_ref[first + full : first + full + 1, part * LOW : part * LOW + tail] = value

    def one(j, carry):
        first = pl.multiple_of(starts[j], chunk)
        at = pl.multiple_of(j * chunk, chunk)
        owner = owner_ref[:, pl.ds(first, chunk)]
        low = lax.broadcasted_iota(jnp.int32, (LOW, chunk), 0) == (owner & (LOW - 1))
        low = low.astype(jnp.bfloat16)
        rows_of = jnp.dot(parts_ref[...], jnp.concatenate([low] * 3, axis=0), preferred_element_type=jnp.float32)
        high = lax.broadcasted_iota(jnp.int32, (rows, chunk), 0) == (owner // LOW)
        for axis in range(3):
            base = jnp.sum(jnp.where(high, rows_of[axis * rows : (axis + 1) * rows], 0.0), axis=0, keepdims=True)
            out_ref[axis : axis + 1, pl.ds(at, chunk)] = base + probe_radius * offset_ref[axis : axis + 1, pl.ds(first, chunk)]
        return carry

    lax.fori_loop(0, count, one, 0, unroll=UNROLL)


def chosen_positions(atom_centers, owner, offsets, starts, chunk):
    count = starts.shape[0]
    atoms = atom_centers.shape[1]
    full = (atoms - 1) // LOW
    rows = -(-(full + 1) // 16) * 16
    table = atom_centers[:, : full * LOW].reshape(3 * full, LOW)
    whole = pl.BlockSpec(memory_space=pltpu.VMEM)
    return pl.pallas_call(
        functools.partial(position_kernel, chunk=chunk, count=count, rows=rows),
        out_shape=jax.ShapeDtypeStruct((3, count * chunk), jnp.float32),
        in_specs=[pl.BlockSpec(memory_space=pltpu.SMEM), whole, whole, whole, whole],
        out_specs=whole,
        scratch_shapes=[pltpu.VMEM((3 * rows, 3 * LOW), jnp.bfloat16)],
        compiler_params=params(24),
        cost_estimate=pl.CostEstimate(flops=2 * 9 * rows * LOW * count * chunk, bytes_accessed=4 * atoms * 3, transcendentals=0),
        name="positions",
    )(starts, table, atom_centers[:, full * LOW :], owner, offsets)


def features(pos, source):
    first, second, third = three_parts(pos)
    x1, x2, x3 = (part.astype(jnp.float32) for part in (first, second, third))
    square_high, square_low, _ = three_parts(x1 * x1)
    rest = 2.0 * (x1 * x2) + (2.0 * (x1 * x3) + x2 * x2) + 2.0 * (x2 * x3)
    rest = rest[0:1] + rest[1:2] + rest[2:3]
    rest = list(three_parts(rest if source else rest + soft_square))
    one = jnp.ones_like(rest[0])
    ones = [one] * 9
    squares = [square_high, square_low, *rest]
    scale = -2.0 if source else 1.0
    parts = [(scale * part).astype(jnp.bfloat16) for part in (x1, x2, x3)]
    large, small = [], []
    for axis in range(3):
        c = slice(axis, axis + 1)
        mine = [square_high[c], square_low[c]]
        large += [parts[0][c], *(mine + [one, one] if source else [one, one] + mine)]
    for pair in [(0, 1), (1, 0), (1, 1), (0, 2), (2, 0), (1, 2), (2, 1), (2, 2)]:
        small.append(parts[pair[0] if source else pair[1]])
    small += rest + [one] * 3 if source else [one] * 3 + rest
    pad = [jnp.zeros_like(one)] * (FEATURES - 45)
    return jnp.concatenate(large + small + pad, axis=0)


def entry_kernel(source_ref, target_ref, *refs):
    out_refs, (source_rows, target_cols) = refs[:-2], refs[-2:]
    n = source_ref.shape[1]
    source_rows[...] = features(source_ref[...], True).T
    target_cols[...] = features(target_ref[...], False)
    n_out, m = out_refs[0].shape
    step, wide = 512, min(m, 1024)
    for piece, out_ref in enumerate(out_refs):

        def one(i, carry, piece=piece, out_ref=out_ref):
            at = pl.multiple_of(i * step, step)
            rows = source_rows[pl.ds(piece * n_out + at, step), :]
            for j in range(0, m, wide):
                dist_sq = jnp.dot(rows, target_cols[:, j : j + wide], preferred_element_type=jnp.float32)
                out_ref[pl.ds(at, step), j : j + wide] = lax.rsqrt(dist_sq).astype(jnp.bfloat16)
            return carry

        lax.fori_loop(0, n_out // step, one, 0)


def entries(source_pos, target_pos, pieces):
    n, m = source_pos.shape[1], target_pos.shape[1]
    whole = pl.BlockSpec(memory_space=pltpu.VMEM)
    return pl.pallas_call(
        entry_kernel,
        out_shape=[jax.ShapeDtypeStruct((n // pieces, m), jnp.bfloat16)] * pieces,
        in_specs=[whole, whole],
        out_specs=[whole] * pieces,
        scratch_shapes=[pltpu.VMEM((n, FEATURES), jnp.bfloat16), pltpu.VMEM((FEATURES, m), jnp.bfloat16)],
        compiler_params=params(32),
        cost_estimate=pl.CostEstimate(flops=12 * n * m, bytes_accessed=2 * n * m, transcendentals=n * m),
        name="entries",
    )(source_pos, target_pos)


def apply_kernel(*refs, pieces, more, first):
    charge_refs, kern_refs, out_ref = refs[:pieces], refs[pieces : 2 * pieces], refs[-1]
    wide = 512
    for j in range(0, out_ref.shape[1], wide):
        total = refs[2 * pieces][:, j : j + wide] if more else None
        for charge_ref, kern_ref in zip(charge_refs, kern_refs):
            kern = kern_ref[:, first + j : first + j + wide]
            part = jnp.dot(charge_ref[...], kern, preferred_element_type=jnp.float32)
            total = part if total is None else total + part
        out_ref[:, j : j + wide] = total


def apply_entries(charges, kerns, total=None, first=0, m=None):
    pieces = len(charges)
    k, n = charges[0].shape
    m = kerns[0].shape[1] if m is None else m
    whole = pl.BlockSpec(memory_space=pltpu.VMEM)
    more = [] if total is None else [total]
    return pl.pallas_call(
        functools.partial(apply_kernel, pieces=pieces, more=bool(more), first=first),
        out_shape=jax.ShapeDtypeStruct((k, m), jnp.float32),
        in_specs=[whole] * (2 * pieces + len(more)),
        out_specs=whole,
        compiler_params=params(32),
        cost_estimate=pl.CostEstimate(flops=8 * k * n * pieces * m, bytes_accessed=2 * pieces * n * m, transcendentals=0),
        name="apply",
    )(*charges, *kerns, *more)


def dots(left, right):
    return lax.dot_general(left, right, (((1,), (1,)), ((), ())), precision=HIGHEST, preferred_element_type=jnp.float32)


def left_t(left, right):
    return lax.dot_general(left, right, (((0,), (0,)), ((), ())), precision=HIGHEST, preferred_element_type=jnp.float32)


def mul(left, right):
    return jnp.dot(left, right, precision=HIGHEST, preferred_element_type=jnp.float32)


def inverse_of_pair(a, b, c):
    scale = 1.0 / (a * c - b * b)
    return c * scale, -b * scale, a * scale


def eliminate_four(system, i, row_of):
    col = [jnp.broadcast_to(system[:, i + j : i + j + 1], system.shape) for j in range(4)]
    row = [system[i + j : i + j + 1, :] for j in range(4)]

    def entry(r, c):
        return col[c][i + r : i + r + 1]

    a, b, d = inverse_of_pair(entry(0, 0), entry(1, 0), entry(1, 1))
    t0, t1 = a * row[0] + b * row[1], b * row[0] + d * row[1]
    b00, b01, b10, b11 = entry(2, 0), entry(3, 0), entry(2, 1), entry(3, 1)
    e00, e10 = a * b00 + b * b10, b * b00 + d * b10
    e01, e11 = a * b01 + b * b11, b * b01 + d * b11
    u, v, w = inverse_of_pair(
        entry(2, 2) - (b00 * e00 + b10 * e10),
        entry(3, 2) - (b00 * e01 + b10 * e11),
        entry(3, 3) - (b01 * e01 + b11 * e11),
    )
    y0, y1 = row[2] - (b00 * t0 + b10 * t1), row[3] - (b01 * t0 + b11 * t1)
    q2, q3 = u * y0 + v * y1, v * y0 + w * y1
    solved = [t0 - (e00 * q2 + e01 * q3), t1 - (e10 * q2 + e11 * q3), q2, q3]
    rest = (system - (col[0] * solved[0] + col[1] * solved[1])) - (col[2] * solved[2] + col[3] * solved[3])
    for j in range(4):
        rest = jnp.where(row_of == i + j, solved[j], rest)
    return rest


def eliminate(systems):
    k = systems[0].shape[0]
    row_of = lax.broadcasted_iota(jnp.int32, systems[0].shape, 0)
    for i in range(0, k, 4):
        systems = [eliminate_four(system, i, row_of) for system in systems]
    return [system[:, k:] for system in systems]


def fold(square):
    half = square.shape[0] // 2
    return jnp.concatenate([square[:half], square[half:]], axis=1)


def unfold(folded):
    k = folded.shape[1] // 2
    return jnp.concatenate([folded[:, :k], folded[:, k:]], axis=0)


def first_gram_kernel(own_ref, other_ref, self_ref, direction_ref, image_ref, gram_ref):
    direction = direction_ref[...]
    image = own_ref[...] + other_ref[...] + self_ref[...] * direction
    image_ref[...] = image
    k = direction.shape[0]
    both = dots(jnp.concatenate([direction, image], axis=0), image)
    gram_ref[:k, :] = jnp.concatenate([both[:k], both[k:]], axis=1)
    gram_ref[k:, :] = fold(dots(direction, direction))


def first_gram(partial, other, self_row, direction):
    k, n = direction.shape
    whole = pl.BlockSpec(memory_space=pltpu.VMEM)
    return pl.pallas_call(
        first_gram_kernel,
        out_shape=[jax.ShapeDtypeStruct((k, n), jnp.float32), jax.ShapeDtypeStruct((k + k // 2, 2 * k), jnp.float32)],
        in_specs=[whole] * 4,
        out_specs=[whole, whole],
        compiler_params=params(8),
        cost_estimate=pl.CostEstimate(flops=6 * 2 * 3 * k * k * n, bytes_accessed=4 * k * n * 4, transcendentals=0),
        name="first_gram",
    )(partial, other, self_row, direction)


def first_update_kernel(*refs, count):
    part_refs, (image_ref, direction_ref, alpha_ref, next_ref, charges_ref) = refs[:count], refs[count:]
    total = sum_of([ref[...] for ref in part_refs])
    k = total.shape[1] // 2
    gram, image_sq, norm = total[:k, :k], total[:k, k:], unfold(total[k:, :])
    norm = 0.5 * (norm + norm.T)
    unit = (lax.broadcasted_iota(jnp.int32, (k, k), 0) == lax.broadcasted_iota(jnp.int32, (k, k), 1)).astype(jnp.float32)
    alpha, inverse = eliminate([
        jnp.concatenate([0.5 * (gram + gram.T), norm], axis=1),
        jnp.concatenate([norm, unit], axis=1),
    ])
    both = mul(jnp.concatenate([gram, image_sq], axis=0), alpha)
    cross = both[:k]
    norm_next = norm - cross - cross.T + left_t(alpha, both[k:])
    beta = mul(inverse, norm_next)
    alpha_ref[:, :k] = alpha
    alpha_ref[:, k:] = norm_next
    direction = direction_ref[...]
    weights = jnp.concatenate([beta, -alpha], axis=0)
    later = direction + left_t(weights, jnp.concatenate([direction, image_ref[...]], axis=0))
    next_ref[...] = later
    charges_ref[...] = later.astype(jnp.bfloat16)


def sum_of(values):
    while len(values) > 1:
        values = [values[i] + values[i + 1] for i in range(0, len(values), 2)]
    return values[0]


def first_update(parts, image, direction):
    k, n = direction.shape
    whole = pl.BlockSpec(memory_space=pltpu.VMEM)
    return pl.pallas_call(
        functools.partial(first_update_kernel, count=len(parts)),
        out_shape=[
            jax.ShapeDtypeStruct((k, 2 * k), jnp.float32),
            jax.ShapeDtypeStruct((k, n), jnp.float32),
            jax.ShapeDtypeStruct((k, n), jnp.bfloat16),
        ],
        in_specs=[whole] * (len(parts) + 2),
        out_specs=[whole] * 3,
        compiler_params=params(16),
        cost_estimate=pl.CostEstimate(flops=6 * 2 * 2 * k * k * n, bytes_accessed=4 * k * n * 5, transcendentals=0),
        name="first_update",
    )(*parts, image, direction)


def second_gram_kernel(own_ref, other_ref, self_ref, direction_ref, image_ref, gram_ref):
    direction = direction_ref[...]
    image = own_ref[...] + other_ref[...] + self_ref[...] * direction
    image_ref[...] = image
    k = direction.shape[0]
    gram_ref[:, :k] = dots(direction, image)
    gram_ref[:, k:] = jnp.zeros((k, k), jnp.float32)


def second_gram(partial, other, self_row, direction):
    k, n = direction.shape
    mine = pl.BlockSpec((k, n), lambda i: (0, 0))
    whole = pl.BlockSpec(memory_space=pltpu.VMEM)
    return pl.pallas_call(
        second_gram_kernel,
        grid=(1,),
        out_shape=[jax.ShapeDtypeStruct((k, n), jnp.float32), jax.ShapeDtypeStruct((k, 2 * k), jnp.float32)],
        in_specs=[mine, whole, whole, whole],
        out_specs=[whole, whole],
        compiler_params=params(16),
        cost_estimate=pl.CostEstimate(flops=6 * 2 * k * k * n, bytes_accessed=4 * k * n * 4, transcendentals=0),
        name="second_gram",
    )(partial, other, self_row, direction)


def first_state_kernel(alpha_ref, direction_ref, image_ref, out_ref):
    k, n = direction_ref.shape
    alpha = alpha_ref[:, :k]
    both = left_t(alpha, jnp.concatenate([direction_ref[...], image_ref[...]], axis=1))
    out_ref[:, :n] = both[:, :n]
    out_ref[:, n:] = direction_ref[...] - both[:, n:]


def first_state(alpha, direction, image):
    k, n = direction.shape
    whole = pl.BlockSpec(memory_space=pltpu.VMEM)
    return pl.pallas_call(
        first_state_kernel,
        out_shape=jax.ShapeDtypeStruct((k, 2 * n), jnp.float32),
        in_specs=[whole] * 3,
        out_specs=whole,
        compiler_params=params(16),
        cost_estimate=pl.CostEstimate(flops=6 * 2 * 2 * k * k * n, bytes_accessed=4 * k * n * 4, transcendentals=0),
        name="first_state",
    )(alpha, direction, image)


def last_update_kernel(*refs, count):
    part_refs = refs[:count]
    alpha_ref, state_ref, direction_ref, image_ref, charge_ref, out_ref = refs[count:]
    total = sum_of([ref[...] for ref in part_refs])
    k = total.shape[0]
    n = direction_ref.shape[1]
    gram = total[:, :k]
    (alpha,) = eliminate([jnp.concatenate([0.5 * (gram + gram.T), alpha_ref[:, k:]], axis=1)])
    both = left_t(alpha, jnp.concatenate([direction_ref[...], image_ref[...]], axis=1))
    charge_ref[...] = state_ref[:, :n] + both[:, :n]
    out_ref[...] = state_ref[:, n:] - both[:, n:]


def last_update(parts, alpha, state, direction, image):
    k, n = direction.shape
    whole = pl.BlockSpec(memory_space=pltpu.VMEM)
    return pl.pallas_call(
        functools.partial(last_update_kernel, count=len(parts)),
        out_shape=[jax.ShapeDtypeStruct((k, n), jnp.float32)] * 2,
        in_specs=[whole] * (len(parts) + 4),
        out_specs=[whole] * 2,
        compiler_params=params(16),
        cost_estimate=pl.CostEstimate(flops=6 * 3 * 2 * k * k * n, bytes_accessed=4 * k * n * 6, transcendentals=0),
        name="last_update",
    )(*parts, alpha, state, direction, image)


def per_device_grouped(right_side, atom_centers, tessera_owner, tessera_angles, self_term):
    columns, shard = right_side.shape
    n_tgt = lax.axis_size("tgt")
    n_src = lax.axis_size("src")
    t = lax.axis_index("tgt")
    s = lax.axis_index("src")
    copies = n_tgt // GROUP
    member = t % GROUP
    ours = t // GROUP
    width = shard * n_src

    def swap(value, bits):
        return lax.ppermute(value, "tgt", [(i, i ^ bits) for i in range(n_tgt)])

    def swap_core(value):
        return lax.ppermute(value, "src", [(0, 1), (1, 0)])

    near = jnp.concatenate([right_side, self_term[None, :]], axis=0)
    far = swap(near, GROUP)
    both = jnp.where(ours == 0, jnp.concatenate([near, far], axis=1), jnp.concatenate([far, near], axis=1))
    direction, self_row = both[:columns], both[columns : columns + 1]
    charges = direction.astype(jnp.bfloat16)
    gathered = [charges] + [swap(charges, bits) for bits in range(1, GROUP)]

    angles = lax.optimization_barrier(tessera_angles.reshape(2, -1, 128))
    offsets = lax.optimization_barrier(unit_offsets(angles)).reshape(3, -1)
    starts = [((member ^ bits) + GROUP * c) * width + s * shard for bits in range(GROUP) for c in range(copies)]
    starts += [(member + GROUP * c) * width + (1 - s) * shard for c in range(copies)]
    pos = chosen_positions(atom_centers, tessera_owner[None, :], offsets, jnp.stack(starts).astype(jnp.int32), shard)
    n_near = copies * shard
    n_all = GROUP * n_near
    target_pos = jnp.concatenate([pos[:, :n_near], pos[:, n_all:]], axis=1)
    kerns = entries(pos[:, :n_all], target_pos, GROUP)

    def group_sum_parts(value):
        value = value + swap_core(value)
        return [value] + [swap(value, bits) for bits in range(1, GROUP)]

    def mine(value):
        return lax.dynamic_slice_in_dim(value, ours * shard, shard, 1)

    to_other = apply_entries(gathered, kerns, first=n_near, m=n_near)
    other = swap_core(to_other)
    image, gram = first_gram(apply_entries(gathered, kerns, m=n_near), other, self_row, direction)
    alpha, later, charges = first_update(group_sum_parts(gram), image, direction)

    gathered = [swap(charges, bits) for bits in range(1, GROUP)]
    partial = apply_entries([charges], kerns[:1])
    for piece, kern in zip(gathered, kerns[1:]):
        partial = apply_entries([piece], [kern], partial)
    state = first_state(alpha, right_side, mine(image))
    image, gram = second_gram(partial, swap_core(partial[:, n_near:]), self_row, later)
    return tuple(last_update(group_sum_parts(gram), alpha, state, mine(later), mine(image)))


def solution(mesh):
    n_tgt, n_src = mesh.shape["tgt"], mesh.shape["src"]

    def run(right_side, atom_centers, tessera_owner, tessera_angles, self_term):
        total = right_side.shape[1]
        stored = 2 * (total // n_src) * (total // GROUP)
        grouped = n_tgt == 2 * GROUP and n_src == 2 and stored <= STORED_LIMIT
        return jax.shard_map(
            per_device_grouped if grouped else per_device_general,
            mesh=mesh,
            in_specs=(P("conf", ("tgt", "src")), P("conf", None), P(), P(), P(("tgt", "src"))),
            out_specs=(P("conf", ("tgt", "src")), P("conf", ("tgt", "src"))),
            check_vma=False,
        )(right_side, atom_centers, tessera_owner, tessera_angles, self_term)

    return run
```

```python
import functools

import jax
import jax.numpy as jnp
from jax import lax
from jax.experimental import pallas as pl
from jax.experimental.pallas import tpu as pltpu
from jax.sharding import PartitionSpec as P

ITERS = 2
GROUP = 4
LOW = 256
FEATURES = 48
UNROLL = 10
BLOCK = 8
STORED_LIMIT = 32 * 2**20

soft_square = 0.09
probe_radius = 0.15
HIGHEST = lax.Precision.HIGHEST
MIB = 2**20


def params(mib, **kw):
    return pltpu.CompilerParams(vmem_limit_bytes=mib * MIB, **kw)


def positions(atom_centers, tessera_owner, tessera_angles):
    base = jnp.take(atom_centers, tessera_owner, axis=1)
    return base + probe_radius * unit_offsets(tessera_angles)


def unit_offsets(tessera_angles):
    azimuth = tessera_angles[0]
    polar = tessera_angles[1]
    sine = jnp.sin(polar)
    return jnp.stack([jnp.cos(azimuth) * sine, jnp.sin(azimuth) * sine, jnp.cos(polar)])


def tile_apply(total, source_pos, charges, target_pos):
    diff = source_pos[0][:, None] - target_pos[0][None, :]
    dist_sq = diff * diff
    diff = source_pos[1][:, None] - target_pos[1][None, :]
    dist_sq = dist_sq + diff * diff
    diff = source_pos[2][:, None] - target_pos[2][None, :]
    dist_sq = dist_sq + diff * diff
    kern = lax.rsqrt(dist_sq + soft_square).astype(jnp.bfloat16)
    return total + jnp.dot(charges, kern, preferred_element_type=jnp.float32)


def products(left, right):
    return lax.dot_general(
        left,
        right,
        (((1,), (1,)), ((), ())),
        precision=HIGHEST,
        preferred_element_type=jnp.float32,
    )


def chol_solve(matrix, rhs):
    lower = jnp.linalg.cholesky(matrix)
    middle = lax.linalg.triangular_solve(lower, rhs, left_side=True, lower=True)
    return lax.linalg.triangular_solve(lower, middle, left_side=True, lower=True, transpose_a=True)


def per_device_general(right_side, atom_centers, tessera_owner, tessera_angles, self_term):
    shard = right_side.shape[1]
    columns = right_side.shape[0]
    n_src = lax.axis_size("src")
    tgt_index = lax.axis_index("tgt")
    src_index = lax.axis_index("src")
    allpos = positions(atom_centers, tessera_owner, tessera_angles)

    def residual_norm(residual):
        return lax.psum(products(residual, residual), ("tgt", "src"))

    solution = jnp.zeros_like(right_side)
    residual = right_side
    direction = right_side
    norm_now = residual_norm(residual)
    for step in range(ITERS):
        charges = direction.astype(jnp.bfloat16)
        width = shard * n_src
        target_pos = lax.dynamic_slice_in_dim(allpos, tgt_index * width, width, 1)
        empty = jnp.zeros((columns, width), jnp.float32)
        piece = lax.all_gather(charges, "tgt", axis=1, tiled=True)
        sub = min(piece.shape[1], shard)
        count = piece.shape[1] // sub

        def one_block(j, acc):
            column = j * sub
            row_first = column // shard * width + src_index * shard + column % shard
            source_pos = lax.dynamic_slice_in_dim(allpos, row_first, sub, 1)
            part = lax.dynamic_slice_in_dim(piece, j * sub, sub, 1)
            return tile_apply(acc, source_pos, part, target_pos)

        partial_value = lax.fori_loop(0, count, one_block, empty)
        near = lax.psum_scatter(partial_value, "src", scatter_dimension=1, tiled=True)
        image = near + self_term[None, :] * direction
        gram = lax.psum(products(direction, image), ("tgt", "src"))
        alpha = chol_solve(gram, norm_now)
        solution = solution + jnp.dot(alpha.T, direction, precision=HIGHEST)
        residual = residual - jnp.dot(alpha.T, image, precision=HIGHEST)
        if step + 1 < ITERS:
            norm_next = residual_norm(residual)
            beta = chol_solve(norm_now, norm_next)
            direction = residual + jnp.dot(beta.T, direction, precision=HIGHEST)
            norm_now = norm_next
    return (solution, residual)


def three_parts(value):
    first = value.astype(jnp.bfloat16)
    rest = value - first.astype(jnp.float32)
    second = rest.astype(jnp.bfloat16)
    third = (rest - second.astype(jnp.float32)).astype(jnp.bfloat16)
    return first, second, third


def position_kernel(
    starts, table_hbm, owner_hbm, offset_ref, out_ref, table_ref, owner_ref, rows_ref, parts_ref, table_sem, owner_sem, *, chunk, count, rows
):
    table_copy = pltpu.make_async_copy(table_hbm, table_ref, table_sem)
    owner_copy = pltpu.make_async_copy(owner_hbm, owner_ref, owner_sem)
    table_copy.start()
    owner_copy.start()
    atoms = table_ref.shape[1]
    last = (atoms - 1) // LOW
    for axis in range(3):
        at = axis * rows + last
        rows_ref[at : (axis + 1) * rows, :] = jnp.zeros((rows - last, LOW), jnp.float32)
    table_copy.wait()
    owner_copy.wait()
    for row in range(last + 1):
        wide = min(LOW, atoms - row * LOW)
        values = table_ref[:, row * LOW : row * LOW + wide]
        for axis in range(3):
            at = axis * rows + row
            rows_ref[at : at + 1, :wide] = values[axis : axis + 1]
    for part, value in enumerate(three_parts(rows_ref[...])):
        parts_ref[:, part * LOW : (part + 1) * LOW] = value

    def one(j, carry):
        first = pl.multiple_of(starts[j], chunk)
        at = pl.multiple_of(j * chunk, chunk)
        owner = owner_ref[:, pl.ds(first, chunk)]
        low = lax.broadcasted_iota(jnp.int32, (LOW, chunk), 0) == (owner & (LOW - 1))
        low = low.astype(jnp.bfloat16)
        rows_of = jnp.dot(parts_ref[...], jnp.concatenate([low] * 3, axis=0), preferred_element_type=jnp.float32)
        high = lax.broadcasted_iota(jnp.int32, (rows, chunk), 0) == (owner // LOW)
        for axis in range(3):
            base = jnp.sum(jnp.where(high, rows_of[axis * rows : (axis + 1) * rows], 0.0), axis=0, keepdims=True)
            out_ref[axis : axis + 1, pl.ds(at, chunk)] = base + probe_radius * offset_ref[axis : axis + 1, pl.ds(first, chunk)]
        return carry

    lax.fori_loop(0, count, one, 0, unroll=UNROLL)


def in_hbm(array):
    return pltpu.with_memory_space_constraint(array, pltpu.HBM)


def chosen_positions(atom_centers, owner, offsets, starts, chunk):
    count = starts.shape[0]
    atoms = atom_centers.shape[1]
    rows = -(-atoms // (16 * LOW)) * 16
    whole = pl.BlockSpec(memory_space=pltpu.VMEM)
    far = pl.BlockSpec(memory_space=pltpu.HBM)
    return pl.pallas_call(
        functools.partial(position_kernel, chunk=chunk, count=count, rows=rows),
        out_shape=jax.ShapeDtypeStruct((3, count * chunk), jnp.float32),
        in_specs=[pl.BlockSpec(memory_space=pltpu.SMEM), far, far, whole],
        out_specs=whole,
        scratch_shapes=[
            pltpu.VMEM(atom_centers.shape, jnp.float32),
            pltpu.VMEM(owner.shape, jnp.int32),
            pltpu.VMEM((3 * rows, LOW), jnp.float32),
            pltpu.VMEM((3 * rows, 3 * LOW), jnp.bfloat16),
            pltpu.SemaphoreType.DMA,
            pltpu.SemaphoreType.DMA,
        ],
        compiler_params=params(24),
        cost_estimate=pl.CostEstimate(flops=2 * 9 * rows * LOW * count * chunk, bytes_accessed=4 * atoms * 3, transcendentals=0),
        name="positions",
    )(starts, in_hbm(atom_centers), in_hbm(owner), offsets)


def features(pos, source):
    first, second, third = three_parts(pos)
    x1, x2, x3 = (part.astype(jnp.float32) for part in (first, second, third))
    square_high, square_low, _ = three_parts(x1 * x1)
    rest = 2.0 * (x1 * x2) + (2.0 * (x1 * x3) + x2 * x2) + 2.0 * (x2 * x3)
    rest = rest[0:1] + rest[1:2] + rest[2:3]
    rest = list(three_parts(rest if source else rest + soft_square))
    one = jnp.ones_like(rest[0])
    ones = [one] * 9
    squares = [square_high, square_low, *rest]
    scale = -2.0 if source else 1.0
    parts = [(scale * part).astype(jnp.bfloat16) for part in (x1, x2, x3)]
    large, small = [], []
    for axis in range(3):
        c = slice(axis, axis + 1)
        mine = [square_high[c], square_low[c]]
        large += [parts[0][c], *(mine + [one, one] if source else [one, one] + mine)]
    for pair in [(0, 1), (1, 0), (1, 1), (0, 2), (2, 0), (1, 2), (2, 1), (2, 2)]:
        small.append(parts[pair[0] if source else pair[1]])
    small += rest + [one] * 3 if source else [one] * 3 + rest
    pad = [jnp.zeros_like(one)] * (FEATURES - 45)
    return jnp.concatenate(large + small + pad, axis=0)


def entry_kernel(source_ref, target_ref, *refs):
    out_refs, (source_rows, target_cols) = refs[:-2], refs[-2:]
    n = source_ref.shape[1]
    source_rows[...] = features(source_ref[...], True).T
    target_cols[...] = features(target_ref[...], False)
    n_out, m = out_refs[0].shape
    step, wide = 512, min(m, 1024)
    for piece, out_ref in enumerate(out_refs):

        def one(i, carry, piece=piece, out_ref=out_ref):
            at = pl.multiple_of(i * step, step)
            rows = source_rows[pl.ds(piece * n_out + at, step), :]
            for j in range(0, m, wide):
                dist_sq = jnp.dot(rows, target_cols[:, j : j + wide], preferred_element_type=jnp.float32)
                out_ref[pl.ds(at, step), j : j + wide] = lax.rsqrt(dist_sq).astype(jnp.bfloat16)
            return carry

        lax.fori_loop(0, n_out // step, one, 0)


def entries(source_pos, target_pos, pieces):
    n, m = source_pos.shape[1], target_pos.shape[1]
    whole = pl.BlockSpec(memory_space=pltpu.VMEM)
    return pl.pallas_call(
        entry_kernel,
        out_shape=[jax.ShapeDtypeStruct((n // pieces, m), jnp.bfloat16)] * pieces,
        in_specs=[whole, whole],
        out_specs=[whole] * pieces,
        scratch_shapes=[pltpu.VMEM((n, FEATURES), jnp.bfloat16), pltpu.VMEM((FEATURES, m), jnp.bfloat16)],
        compiler_params=params(32),
        cost_estimate=pl.CostEstimate(flops=12 * n * m, bytes_accessed=2 * n * m, transcendentals=n * m),
        name="entries",
    )(source_pos, target_pos)


def apply_kernel(*refs, pieces, more, first):
    charge_refs, kern_refs, out_ref = refs[:pieces], refs[pieces : 2 * pieces], refs[-1]
    wide = 512
    for j in range(0, out_ref.shape[1], wide):
        total = refs[2 * pieces][:, j : j + wide] if more else None
        for charge_ref, kern_ref in zip(charge_refs, kern_refs):
            kern = kern_ref[:, first + j : first + j + wide]
            part = jnp.dot(charge_ref[...], kern, preferred_element_type=jnp.float32)
            total = part if total is None else total + part
        out_ref[:, j : j + wide] = total


def apply_entries(charges, kerns, total=None, first=0, m=None):
    pieces = len(charges)
    k, n = charges[0].shape
    m = kerns[0].shape[1] if m is None else m
    whole = pl.BlockSpec(memory_space=pltpu.VMEM)
    more = [] if total is None else [total]
    return pl.pallas_call(
        functools.partial(apply_kernel, pieces=pieces, more=bool(more), first=first),
        out_shape=jax.ShapeDtypeStruct((k, m), jnp.float32),
        in_specs=[whole] * (2 * pieces + len(more)),
        out_specs=whole,
        compiler_params=params(32),
        cost_estimate=pl.CostEstimate(flops=k * n, bytes_accessed=n, transcendentals=0),
        name="apply",
    )(*charges, *kerns, *more)


def dots(left, right):
    return lax.dot_general(left, right, (((1,), (1,)), ((), ())), precision=HIGHEST, preferred_element_type=jnp.float32)


def left_t(left, right):
    return lax.dot_general(left, right, (((0,), (0,)), ((), ())), precision=HIGHEST, preferred_element_type=jnp.float32)


def mul(left, right):
    return jnp.dot(left, right, precision=HIGHEST, preferred_element_type=jnp.float32)


def inverse_of_pair(a, b, c):
    scale = 1.0 / (a * c - b * b)
    return c * scale, -b * scale, a * scale


def eliminate_block(system, first, row_of):
    col = [jnp.broadcast_to(system[:, first + j : first + j + 1], system.shape) for j in range(BLOCK)]
    row = [system[first + j : first + j + 1, :] for j in range(BLOCK)]
    lower = {(r, c): col[c][first + r : first + r + 1] for c in range(BLOCK) for r in range(c, BLOCK)}

    def entry(r, c):
        return lower[max(r, c), min(r, c)]

    inverses = []
    for p in range(0, BLOCK, 2):
        a, b, d = inverse_of_pair(entry(p, p), entry(p + 1, p), entry(p + 1, p + 1))
        inverses.append((a, b, d))
        for r in range(BLOCK - 1, p + 1, -1):
            x, y = entry(r, p), entry(r, p + 1)
            f0, f1 = x * a + y * b, x * b + y * d
            for c in range(p + 2, r + 1):
                lower[r, c] = lower[r, c] - (f0 * entry(c, p) + f1 * entry(c, p + 1))
            row[r] = row[r] - (f0 * row[p] + f1 * row[p + 1])
    solved = [None] * BLOCK
    for p in range(BLOCK - 2, -1, -2):
        y0, y1 = row[p], row[p + 1]
        for c in range(p + 2, BLOCK):
            y0, y1 = y0 - entry(c, p) * solved[c], y1 - entry(c, p + 1) * solved[c]
        a, b, d = inverses[p // 2]
        solved[p], solved[p + 1] = a * y0 + b * y1, b * y0 + d * y1
    rest = system
    for j in range(0, BLOCK, 2):
        rest = rest - (col[j] * solved[j] + col[j + 1] * solved[j + 1])
    for j in range(BLOCK):
        rest = jnp.where(row_of == first + j, solved[j], rest)
    return rest


def eliminate(systems):
    k = systems[0].shape[0]
    row_of = lax.broadcasted_iota(jnp.int32, systems[0].shape, 0)
    for first in range(0, k, BLOCK):
        systems = [eliminate_block(system, first, row_of) for system in systems]
    return [system[:, k:] for system in systems]


def fold(square):
    half = square.shape[0] // 2
    return jnp.concatenate([square[:half], square[half:]], axis=1)


def unfold(folded):
    k = folded.shape[1] // 2
    return jnp.concatenate([folded[:, :k], folded[:, k:]], axis=0)


def first_gram_kernel(own_ref, other_ref, self_ref, direction_ref, image_ref, gram_ref):
    direction = direction_ref[...]
    image = own_ref[...] + other_ref[...] + self_ref[...] * direction
    image_ref[...] = image
    k = direction.shape[0]
    both = dots(jnp.concatenate([direction, image], axis=0), image)
    gram_ref[:k, :] = jnp.concatenate([both[:k], both[k:]], axis=1)
    gram_ref[k:, :] = fold(dots(direction, direction))


def first_gram(partial, other, self_row, direction):
    k, n = direction.shape
    whole = pl.BlockSpec(memory_space=pltpu.VMEM)
    return pl.pallas_call(
        first_gram_kernel,
        out_shape=[jax.ShapeDtypeStruct((k, n), jnp.float32), jax.ShapeDtypeStruct((k + k // 2, 2 * k), jnp.float32)],
        in_specs=[whole] * 4,
        out_specs=[whole, whole],
        compiler_params=params(8),
        cost_estimate=pl.CostEstimate(flops=6 * 2 * 3 * k * k * n, bytes_accessed=4 * k * n * 4, transcendentals=0),
        name="first_gram",
    )(partial, other, self_row, direction)


def first_update_kernel(*refs, count):
    part_refs, (image_ref, direction_ref, alpha_ref, next_ref, charges_ref) = refs[:count], refs[count:]
    total = sum_of([ref[...] for ref in part_refs])
    k = total.shape[1] // 2
    gram, image_sq, norm = total[:k, :k], total[:k, k:], unfold(total[k:, :])
    norm = 0.5 * (norm + norm.T)
    unit = (lax.broadcasted_iota(jnp.int32, (k, k), 0) == lax.broadcasted_iota(jnp.int32, (k, k), 1)).astype(jnp.float32)
    alpha, inverse = eliminate([
        jnp.concatenate([0.5 * (gram + gram.T), norm], axis=1),
        jnp.concatenate([norm, unit], axis=1),
    ])
    both = mul(jnp.concatenate([gram, image_sq], axis=0), alpha)
    cross = both[:k]
    norm_next = norm - cross - cross.T + left_t(alpha, both[k:])
    beta = mul(inverse, norm_next)
    alpha_ref[:, :k] = alpha
    alpha_ref[:, k:] = norm_next
    direction = direction_ref[...]
    weights = jnp.concatenate([beta, -alpha], axis=0)
    later = direction + left_t(weights, jnp.concatenate([direction, image_ref[...]], axis=0))
    next_ref[...] = later
    charges_ref[...] = later.astype(jnp.bfloat16)


def sum_of(values):
    while len(values) > 1:
        values = [values[i] + values[i + 1] for i in range(0, len(values), 2)]
    return values[0]


def first_update(parts, image, direction):
    k, n = direction.shape
    whole = pl.BlockSpec(memory_space=pltpu.VMEM)
    return pl.pallas_call(
        functools.partial(first_update_kernel, count=len(parts)),
        out_shape=[
            jax.ShapeDtypeStruct((k, 2 * k), jnp.float32),
            jax.ShapeDtypeStruct((k, n), jnp.float32),
            jax.ShapeDtypeStruct((k, n), jnp.bfloat16),
        ],
        in_specs=[whole] * (len(parts) + 2),
        out_specs=[whole] * 3,
        compiler_params=params(16),
        cost_estimate=pl.CostEstimate(flops=6 * 2 * 2 * k * k * n, bytes_accessed=4 * k * n * 5, transcendentals=0),
        name="first_update",
    )(*parts, image, direction)


def second_gram_kernel(own_ref, other_ref, self_ref, direction_ref, image_ref, gram_ref):
    direction = direction_ref[...]
    image = own_ref[...] + other_ref[...] + self_ref[...] * direction
    image_ref[...] = image
    k = direction.shape[0]
    gram_ref[:, :k] = dots(direction, image)
    gram_ref[:, k:] = jnp.zeros((k, k), jnp.float32)


def second_gram(partial, other, self_row, direction):
    k, n = direction.shape
    mine = pl.BlockSpec((k, n), lambda i: (0, 0))
    whole = pl.BlockSpec(memory_space=pltpu.VMEM)
    return pl.pallas_call(
        second_gram_kernel,
        grid=(1,),
        out_shape=[jax.ShapeDtypeStruct((k, n), jnp.float32), jax.ShapeDtypeStruct((k, 2 * k), jnp.float32)],
        in_specs=[mine, whole, whole, whole],
        out_specs=[whole, whole],
        compiler_params=params(16),
        cost_estimate=pl.CostEstimate(flops=6 * 2 * k * k * n, bytes_accessed=4 * k * n * 4, transcendentals=0),
        name="second_gram",
    )(partial, other, self_row, direction)


def first_state_kernel(alpha_ref, direction_ref, image_ref, out_ref):
    k, n = direction_ref.shape
    alpha = alpha_ref[:, :k]
    both = left_t(alpha, jnp.concatenate([direction_ref[...], image_ref[...]], axis=1))
    out_ref[:, :n] = both[:, :n]
    out_ref[:, n:] = direction_ref[...] - both[:, n:]


def first_state(alpha, direction, image):
    k, n = direction.shape
    whole = pl.BlockSpec(memory_space=pltpu.VMEM)
    return pl.pallas_call(
        first_state_kernel,
        out_shape=jax.ShapeDtypeStruct((k, 2 * n), jnp.float32),
        in_specs=[whole] * 3,
        out_specs=whole,
        compiler_params=params(16),
        cost_estimate=pl.CostEstimate(flops=6 * 2 * 2 * k * k * n, bytes_accessed=4 * k * n * 4, transcendentals=0),
        name="first_state",
    )(alpha, direction, image)


def last_update_kernel(*refs, count):
    part_refs = refs[:count]
    alpha_ref, state_ref, direction_ref, image_ref, charge_ref, out_ref = refs[count:]
    total = sum_of([ref[...] for ref in part_refs])
    k = total.shape[0]
    n = direction_ref.shape[1]
    gram = total[:, :k]
    (alpha,) = eliminate([jnp.concatenate([0.5 * (gram + gram.T), alpha_ref[:, k:]], axis=1)])
    both = left_t(alpha, jnp.concatenate([direction_ref[...], image_ref[...]], axis=1))
    charge_ref[...] = state_ref[:, :n] + both[:, :n]
    out_ref[...] = state_ref[:, n:] - both[:, n:]


def last_update(parts, alpha, state, direction, image):
    k, n = direction.shape
    whole = pl.BlockSpec(memory_space=pltpu.VMEM)
    return pl.pallas_call(
        functools.partial(last_update_kernel, count=len(parts)),
        out_shape=[jax.ShapeDtypeStruct((k, n), jnp.float32)] * 2,
        in_specs=[whole] * (len(parts) + 4),
        out_specs=[whole] * 2,
        compiler_params=params(16),
        cost_estimate=pl.CostEstimate(flops=6 * 3 * 2 * k * k * n, bytes_accessed=4 * k * n * 6, transcendentals=0),
        name="last_update",
    )(*parts, alpha, state, direction, image)


def per_device_grouped(right_side, atom_centers, tessera_owner, tessera_angles, self_term):
    columns, shard = right_side.shape
    n_tgt = lax.axis_size("tgt")
    n_src = lax.axis_size("src")
    t = lax.axis_index("tgt")
    s = lax.axis_index("src")
    copies = n_tgt // GROUP
    member = t % GROUP
    ours = t // GROUP
    width = shard * n_src

    def swap(value, bits):
        return lax.ppermute(value, "tgt", [(i, i ^ bits) for i in range(n_tgt)])

    def swap_core(value):
        return lax.ppermute(value, "src", [(0, 1), (1, 0)])

    angles = lax.optimization_barrier(tessera_angles.reshape(2, -1, 128))
    offsets = lax.optimization_barrier(unit_offsets(angles)).reshape(3, -1)
    starts = [((member ^ bits) + GROUP * c) * width + s * shard for bits in range(GROUP) for c in range(copies)]
    starts += [(member + GROUP * c) * width + (1 - s) * shard for c in range(copies)]
    pos = chosen_positions(atom_centers, tessera_owner[None, :], offsets, jnp.stack(starts).astype(jnp.int32), shard)
    n_near = copies * shard
    n_all = GROUP * n_near
    target_pos = jnp.concatenate([pos[:, :n_near], pos[:, n_all:]], axis=1)
    kerns = entries(pos[:, :n_near], target_pos, 1)

    def beside(near, far):
        return jnp.where(ours == 0, jnp.concatenate([near, far], axis=1), jnp.concatenate([far, near], axis=1))

    self_near = self_term[None, :]
    right_far, self_far, kerns = lax.optimization_barrier((swap(right_side, GROUP), swap(self_near, GROUP), kerns))
    direction = beside(right_side, right_far)
    self_row = beside(self_near, self_far)
    charges = direction.astype(jnp.bfloat16)
    gathered = [charges] + [swap(charges, bits) for bits in range(1, GROUP)]
    kerns = [*kerns, *entries(pos[:, n_near:n_all], target_pos, GROUP - 1)]

    def group_sum_parts(value):
        value = value + swap_core(value)
        return [value] + [swap(value, bits) for bits in range(1, GROUP)]

    def mine(value):
        return lax.dynamic_slice_in_dim(value, ours * shard, shard, 1)

    to_other = apply_entries(gathered, kerns, first=n_near, m=n_near)
    other = swap_core(to_other)
    image, gram = first_gram(apply_entries(gathered, kerns, m=n_near), other, self_row, direction)
    alpha, later, charges = first_update(group_sum_parts(gram), image, direction)

    gathered = [swap(charges, bits) for bits in range(1, GROUP)]
    partial = apply_entries([charges], kerns[:1])
    for piece, kern in zip(gathered, kerns[1:]):
        partial = apply_entries([piece], [kern], partial)
    state = first_state(alpha, right_side, mine(image))
    image, gram = second_gram(partial, swap_core(partial[:, n_near:]), self_row, later)
    return tuple(last_update(group_sum_parts(gram), alpha, state, mine(later), mine(image)))


def solution(mesh):
    n_tgt, n_src = mesh.shape["tgt"], mesh.shape["src"]

    def run(right_side, atom_centers, tessera_owner, tessera_angles, self_term):
        total = right_side.shape[1]
        stored = 2 * (total // n_src) * (total // GROUP)
        grouped = n_tgt == 2 * GROUP and n_src == 2 and stored <= STORED_LIMIT
        return jax.shard_map(
            per_device_grouped if grouped else per_device_general,
            mesh=mesh,
            in_specs=(P("conf", ("tgt", "src")), P("conf", None), P(), P(), P(("tgt", "src"))),
            out_specs=(P("conf", ("tgt", "src")), P("conf", ("tgt", "src"))),
            check_vma=False,
        )(right_side, atom_centers, tessera_owner, tessera_angles, self_term)

    return run
```

```python
import functools

import jax
import jax.numpy as jnp
from jax import lax
from jax.experimental import pallas as pl
from jax.experimental.pallas import tpu as pltpu
from jax.sharding import PartitionSpec as P

ITERS = 2
GROUP = 4
LOW = 256
FEATURES = 48
UNROLL = 10
BLOCK = 8
STORED_LIMIT = 32 * 2**20

soft_square = 0.09
probe_radius = 0.15
HIGHEST = lax.Precision.HIGHEST
MIB = 2**20


def params(mib, **kw):
    return pltpu.CompilerParams(vmem_limit_bytes=mib * MIB, **kw)


def positions(atom_centers, tessera_owner, tessera_angles):
    base = jnp.take(atom_centers, tessera_owner, axis=1)
    return base + probe_radius * unit_offsets(tessera_angles)


def unit_offsets(tessera_angles):
    azimuth = tessera_angles[0]
    polar = tessera_angles[1]
    sine = jnp.sin(polar)
    return jnp.stack([jnp.cos(azimuth) * sine, jnp.sin(azimuth) * sine, jnp.cos(polar)])


def tile_apply(total, source_pos, charges, target_pos):
    diff = source_pos[0][:, None] - target_pos[0][None, :]
    dist_sq = diff * diff
    diff = source_pos[1][:, None] - target_pos[1][None, :]
    dist_sq = dist_sq + diff * diff
    diff = source_pos[2][:, None] - target_pos[2][None, :]
    dist_sq = dist_sq + diff * diff
    kern = lax.rsqrt(dist_sq + soft_square).astype(jnp.bfloat16)
    return total + jnp.dot(charges, kern, preferred_element_type=jnp.float32)


def products(left, right):
    return lax.dot_general(
        left,
        right,
        (((1,), (1,)), ((), ())),
        precision=HIGHEST,
        preferred_element_type=jnp.float32,
    )


def chol_solve(matrix, rhs):
    lower = jnp.linalg.cholesky(matrix)
    middle = lax.linalg.triangular_solve(lower, rhs, left_side=True, lower=True)
    return lax.linalg.triangular_solve(lower, middle, left_side=True, lower=True, transpose_a=True)


def per_device_general(right_side, atom_centers, tessera_owner, tessera_angles, self_term):
    shard = right_side.shape[1]
    columns = right_side.shape[0]
    n_src = lax.axis_size("src")
    tgt_index = lax.axis_index("tgt")
    src_index = lax.axis_index("src")
    allpos = positions(atom_centers, tessera_owner, tessera_angles)

    def residual_norm(residual):
        return lax.psum(products(residual, residual), ("tgt", "src"))

    solution = jnp.zeros_like(right_side)
    residual = right_side
    direction = right_side
    norm_now = residual_norm(residual)
    for step in range(ITERS):
        charges = direction.astype(jnp.bfloat16)
        width = shard * n_src
        target_pos = lax.dynamic_slice_in_dim(allpos, tgt_index * width, width, 1)
        empty = jnp.zeros((columns, width), jnp.float32)
        piece = lax.all_gather(charges, "tgt", axis=1, tiled=True)
        sub = min(piece.shape[1], shard)
        count = piece.shape[1] // sub

        def one_block(j, acc):
            column = j * sub
            row_first = column // shard * width + src_index * shard + column % shard
            source_pos = lax.dynamic_slice_in_dim(allpos, row_first, sub, 1)
            part = lax.dynamic_slice_in_dim(piece, j * sub, sub, 1)
            return tile_apply(acc, source_pos, part, target_pos)

        partial_value = lax.fori_loop(0, count, one_block, empty)
        near = lax.psum_scatter(partial_value, "src", scatter_dimension=1, tiled=True)
        image = near + self_term[None, :] * direction
        gram = lax.psum(products(direction, image), ("tgt", "src"))
        alpha = chol_solve(gram, norm_now)
        solution = solution + jnp.dot(alpha.T, direction, precision=HIGHEST)
        residual = residual - jnp.dot(alpha.T, image, precision=HIGHEST)
        if step + 1 < ITERS:
            norm_next = residual_norm(residual)
            beta = chol_solve(norm_now, norm_next)
            direction = residual + jnp.dot(beta.T, direction, precision=HIGHEST)
            norm_now = norm_next
    return (solution, residual)


def three_parts(value):
    first = value.astype(jnp.bfloat16)
    rest = value - first.astype(jnp.float32)
    second = rest.astype(jnp.bfloat16)
    third = (rest - second.astype(jnp.float32)).astype(jnp.bfloat16)
    return first, second, third


def position_kernel(
    starts, table_hbm, owner_hbm, offset_ref, out_ref, table_ref, owner_ref, rows_ref, parts_ref, table_sem, owner_sem, *, chunk, count, rows
):
    table_copy = pltpu.make_async_copy(table_hbm, table_ref, table_sem)
    owner_copy = pltpu.make_async_copy(owner_hbm, owner_ref, owner_sem)
    table_copy.start()
    owner_copy.start()
    atoms = table_ref.shape[1]
    last = (atoms - 1) // LOW
    for axis in range(3):
        at = axis * rows + last
        rows_ref[at : (axis + 1) * rows, :] = jnp.zeros((rows - last, LOW), jnp.float32)
    table_copy.wait()
    owner_copy.wait()
    for row in range(last + 1):
        wide = min(LOW, atoms - row * LOW)
        values = table_ref[:, row * LOW : row * LOW + wide]
        for axis in range(3):
            at = axis * rows + row
            rows_ref[at : at + 1, :wide] = values[axis : axis + 1]
    for part, value in enumerate(three_parts(rows_ref[...])):
        parts_ref[:, part * LOW : (part + 1) * LOW] = value

    def one(j, carry):
        first = pl.multiple_of(starts[j], chunk)
        at = pl.multiple_of(j * chunk, chunk)
        owner = owner_ref[:, pl.ds(first, chunk)]
        low = lax.broadcasted_iota(jnp.int32, (LOW, chunk), 0) == (owner & (LOW - 1))
        low = low.astype(jnp.bfloat16)
        rows_of = jnp.dot(parts_ref[...], jnp.concatenate([low] * 3, axis=0), preferred_element_type=jnp.float32)
        high = lax.broadcasted_iota(jnp.int32, (rows, chunk), 0) == (owner // LOW)
        for axis in range(3):
            base = jnp.sum(jnp.where(high, rows_of[axis * rows : (axis + 1) * rows], 0.0), axis=0, keepdims=True)
            out_ref[axis : axis + 1, pl.ds(at, chunk)] = base + probe_radius * offset_ref[axis : axis + 1, pl.ds(first, chunk)]
        return carry

    lax.fori_loop(0, count, one, 0, unroll=UNROLL)


def in_hbm(array):
    return pltpu.with_memory_space_constraint(array, pltpu.HBM)


def chosen_positions(atom_centers, owner, offsets, starts, chunk):
    count = starts.shape[0]
    atoms = atom_centers.shape[1]
    rows = -(-atoms // (16 * LOW)) * 16
    whole = pl.BlockSpec(memory_space=pltpu.VMEM)
    far = pl.BlockSpec(memory_space=pltpu.HBM)
    return pl.pallas_call(
        functools.partial(position_kernel, chunk=chunk, count=count, rows=rows),
        out_shape=jax.ShapeDtypeStruct((3, count * chunk), jnp.float32),
        in_specs=[pl.BlockSpec(memory_space=pltpu.SMEM), far, far, whole],
        out_specs=whole,
        scratch_shapes=[
            pltpu.VMEM(atom_centers.shape, jnp.float32),
            pltpu.VMEM(owner.shape, jnp.int32),
            pltpu.VMEM((3 * rows, LOW), jnp.float32),
            pltpu.VMEM((3 * rows, 3 * LOW), jnp.bfloat16),
            pltpu.SemaphoreType.DMA,
            pltpu.SemaphoreType.DMA,
        ],
        compiler_params=params(24),
        cost_estimate=pl.CostEstimate(flops=2 * 9 * rows * LOW * count * chunk, bytes_accessed=4 * atoms * 3, transcendentals=0),
        name="positions",
    )(starts, in_hbm(atom_centers), in_hbm(owner), offsets)


def features(pos, source):
    first, second, third = three_parts(pos)
    x1, x2, x3 = (part.astype(jnp.float32) for part in (first, second, third))
    square_high, square_low, _ = three_parts(x1 * x1)
    rest = 2.0 * (x1 * x2) + (2.0 * (x1 * x3) + x2 * x2) + 2.0 * (x2 * x3)
    rest = rest[0:1] + rest[1:2] + rest[2:3]
    rest = list(three_parts(rest if source else rest + soft_square))
    one = jnp.ones_like(rest[0])
    ones = [one] * 9
    squares = [square_high, square_low, *rest]
    scale = -2.0 if source else 1.0
    parts = [(scale * part).astype(jnp.bfloat16) for part in (x1, x2, x3)]
    large, small = [], []
    for axis in range(3):
        c = slice(axis, axis + 1)
        mine = [square_high[c], square_low[c]]
        large += [parts[0][c], *(mine + [one, one] if source else [one, one] + mine)]
    for pair in [(0, 1), (1, 0), (1, 1), (0, 2), (2, 0), (1, 2), (2, 1), (2, 2)]:
        small.append(parts[pair[0] if source else pair[1]])
    small += rest + [one] * 3 if source else [one] * 3 + rest
    pad = [jnp.zeros_like(one)] * (FEATURES - 45)
    return jnp.concatenate(large + small + pad, axis=0)


def entry_kernel(source_ref, target_ref, *refs):
    out_refs, (source_rows, target_cols) = refs[:-2], refs[-2:]
    n = source_ref.shape[1]
    source_rows[...] = features(source_ref[...], True).T
    target_cols[...] = features(target_ref[...], False)
    n_out, m = out_refs[0].shape
    step, wide = 512, min(m, 1024)
    for piece, out_ref in enumerate(out_refs):

        def one(i, carry, piece=piece, out_ref=out_ref):
            at = pl.multiple_of(i * step, step)
            rows = source_rows[pl.ds(piece * n_out + at, step), :]
            for j in range(0, m, wide):
                dist_sq = jnp.dot(rows, target_cols[:, j : j + wide], preferred_element_type=jnp.float32)
                out_ref[pl.ds(at, step), j : j + wide] = lax.rsqrt(dist_sq).astype(jnp.bfloat16)
            return carry

        lax.fori_loop(0, n_out // step, one, 0)


def entries(source_pos, target_pos, pieces):
    n, m = source_pos.shape[1], target_pos.shape[1]
    whole = pl.BlockSpec(memory_space=pltpu.VMEM)
    return pl.pallas_call(
        entry_kernel,
        out_shape=[jax.ShapeDtypeStruct((n // pieces, m), jnp.bfloat16)] * pieces,
        in_specs=[whole, whole],
        out_specs=[whole] * pieces,
        scratch_shapes=[pltpu.VMEM((n, FEATURES), jnp.bfloat16), pltpu.VMEM((FEATURES, m), jnp.bfloat16)],
        compiler_params=params(32),
        cost_estimate=pl.CostEstimate(flops=12 * n * m, bytes_accessed=2 * n * m, transcendentals=n * m),
        name="entries",
    )(source_pos, target_pos)


def apply_kernel(*refs, pieces, more, first):
    charge_refs, kern_refs, out_ref = refs[:pieces], refs[pieces : 2 * pieces], refs[-1]
    wide = 512
    for j in range(0, out_ref.shape[1], wide):
        total = refs[2 * pieces][:, j : j + wide] if more else None
        for charge_ref, kern_ref in zip(charge_refs, kern_refs):
            kern = kern_ref[:, first + j : first + j + wide]
            part = jnp.dot(charge_ref[...], kern, preferred_element_type=jnp.float32)
            total = part if total is None else total + part
        out_ref[:, j : j + wide] = total


def apply_entries(charges, kerns, total=None, first=0, m=None):
    pieces = len(charges)
    k, n = charges[0].shape
    m = kerns[0].shape[1] if m is None else m
    whole = pl.BlockSpec(memory_space=pltpu.VMEM)
    more = [] if total is None else [total]
    return pl.pallas_call(
        functools.partial(apply_kernel, pieces=pieces, more=bool(more), first=first),
        out_shape=jax.ShapeDtypeStruct((k, m), jnp.float32),
        in_specs=[whole] * (2 * pieces + len(more)),
        out_specs=whole,
        compiler_params=params(32),
        cost_estimate=pl.CostEstimate(flops=k * n, bytes_accessed=n, transcendentals=0),
        name="apply",
    )(*charges, *kerns, *more)


def dots(left, right):
    return lax.dot_general(left, right, (((1,), (1,)), ((), ())), precision=HIGHEST, preferred_element_type=jnp.float32)


def left_t(left, right):
    return lax.dot_general(left, right, (((0,), (0,)), ((), ())), precision=HIGHEST, preferred_element_type=jnp.float32)


def mul(left, right):
    return jnp.dot(left, right, precision=HIGHEST, preferred_element_type=jnp.float32)


def inverse_of_pair(a, b, c):
    scale = 1.0 / (a * c - b * b)
    return c * scale, -b * scale, a * scale


def eliminate_block(system, first, row_of):
    col = [jnp.broadcast_to(system[:, first + j : first + j + 1], system.shape) for j in range(BLOCK)]
    row = [system[first + j : first + j + 1, :] for j in range(BLOCK)]
    lower = {(r, c): col[c][first + r : first + r + 1] for c in range(BLOCK) for r in range(c, BLOCK)}

    def entry(r, c):
        return lower[max(r, c), min(r, c)]

    inverses = []
    for p in range(0, BLOCK, 2):
        a, b, d = inverse_of_pair(entry(p, p), entry(p + 1, p), entry(p + 1, p + 1))
        inverses.append((a, b, d))
        for r in range(BLOCK - 1, p + 1, -1):
            x, y = entry(r, p), entry(r, p + 1)
            f0, f1 = x * a + y * b, x * b + y * d
            for c in range(p + 2, r + 1):
                lower[r, c] = lower[r, c] - (f0 * entry(c, p) + f1 * entry(c, p + 1))
            row[r] = row[r] - (f0 * row[p] + f1 * row[p + 1])
    solved = [None] * BLOCK
    for p in range(BLOCK - 2, -1, -2):
        y0, y1 = row[p], row[p + 1]
        for c in range(p + 2, BLOCK):
            y0, y1 = y0 - entry(c, p) * solved[c], y1 - entry(c, p + 1) * solved[c]
        a, b, d = inverses[p // 2]
        solved[p], solved[p + 1] = a * y0 + b * y1, b * y0 + d * y1
    rest = system
    for j in range(0, BLOCK, 2):
        rest = rest - (col[j] * solved[j] + col[j + 1] * solved[j + 1])
    for j in range(BLOCK):
        rest = jnp.where(row_of == first + j, solved[j], rest)
    return rest


def eliminate(systems):
    k = systems[0].shape[0]
    row_of = lax.broadcasted_iota(jnp.int32, systems[0].shape, 0)
    for first in range(0, k, BLOCK):
        systems = [eliminate_block(system, first, row_of) for system in systems]
    return [system[:, k:] for system in systems]


def fold(square):
    half = square.shape[0] // 2
    return jnp.concatenate([square[:half], square[half:]], axis=1)


def unfold(folded):
    k = folded.shape[1] // 2
    return jnp.concatenate([folded[:, :k], folded[:, k:]], axis=0)


def first_gram_kernel(own_ref, other_ref, self_ref, direction_ref, image_ref, gram_ref):
    direction = direction_ref[...]
    image = own_ref[...] + other_ref[...] + self_ref[...] * direction
    image_ref[...] = image
    k = direction.shape[0]
    both = dots(jnp.concatenate([direction, image], axis=0), image)
    gram_ref[:k, :] = jnp.concatenate([both[:k], both[k:]], axis=1)
    gram_ref[k:, :] = fold(dots(direction, direction))


def first_gram(partial, other, self_row, direction):
    k, n = direction.shape
    whole = pl.BlockSpec(memory_space=pltpu.VMEM)
    return pl.pallas_call(
        first_gram_kernel,
        out_shape=[jax.ShapeDtypeStruct((k, n), jnp.float32), jax.ShapeDtypeStruct((k + k // 2, 2 * k), jnp.float32)],
        in_specs=[whole] * 4,
        out_specs=[whole, whole],
        compiler_params=params(8),
        cost_estimate=pl.CostEstimate(flops=6 * 2 * 3 * k * k * n, bytes_accessed=4 * k * n * 4, transcendentals=0),
        name="first_gram",
    )(partial, other, self_row, direction)


def first_update_kernel(*refs, count):
    part_refs, (image_ref, direction_ref, alpha_ref, next_ref, charges_ref) = refs[:count], refs[count:]
    total = sum_of([ref[...] for ref in part_refs])
    k = total.shape[1] // 2
    gram, image_sq, norm = total[:k, :k], total[:k, k:], unfold(total[k:, :])
    norm = 0.5 * (norm + norm.T)
    unit = (lax.broadcasted_iota(jnp.int32, (k, k), 0) == lax.broadcasted_iota(jnp.int32, (k, k), 1)).astype(jnp.float32)
    alpha, inverse = eliminate([
        jnp.concatenate([0.5 * (gram + gram.T), norm], axis=1),
        jnp.concatenate([norm, unit], axis=1),
    ])
    both = mul(jnp.concatenate([gram, image_sq], axis=0), alpha)
    cross = both[:k]
    norm_next = norm - cross - cross.T + left_t(alpha, both[k:])
    beta = mul(inverse, norm_next)
    alpha_ref[:, :k] = alpha
    alpha_ref[:, k:] = norm_next
    direction = direction_ref[...]
    weights = jnp.concatenate([beta, -alpha], axis=0)
    later = direction + left_t(weights, jnp.concatenate([direction, image_ref[...]], axis=0))
    next_ref[...] = later
    charges_ref[...] = later.astype(jnp.bfloat16)


def sum_of(values):
    while len(values) > 1:
        values = [values[i] + values[i + 1] for i in range(0, len(values), 2)]
    return values[0]


def first_update(parts, image, direction):
    k, n = direction.shape
    whole = pl.BlockSpec(memory_space=pltpu.VMEM)
    return pl.pallas_call(
        functools.partial(first_update_kernel, count=len(parts)),
        out_shape=[
            jax.ShapeDtypeStruct((k, 2 * k), jnp.float32),
            jax.ShapeDtypeStruct((k, n), jnp.float32),
            jax.ShapeDtypeStruct((k, n), jnp.bfloat16),
        ],
        in_specs=[whole] * (len(parts) + 2),
        out_specs=[whole] * 3,
        compiler_params=params(16),
        cost_estimate=pl.CostEstimate(flops=6 * 2 * 2 * k * k * n, bytes_accessed=4 * k * n * 5, transcendentals=0),
        name="first_update",
    )(*parts, image, direction)


def second_gram_kernel(own_ref, other_ref, self_ref, direction_ref, image_ref, gram_ref):
    direction = direction_ref[...]
    image = own_ref[...] + other_ref[...] + self_ref[...] * direction
    image_ref[...] = image
    k = direction.shape[0]
    gram_ref[...] = fold(dots(direction, image))


def second_gram(partial, other, self_row, direction):
    k, n = direction.shape
    mine = pl.BlockSpec((k, n), lambda i: (0, 0))
    whole = pl.BlockSpec(memory_space=pltpu.VMEM)
    return pl.pallas_call(
        second_gram_kernel,
        grid=(1,),
        out_shape=[jax.ShapeDtypeStruct((k, n), jnp.float32), jax.ShapeDtypeStruct((k // 2, 2 * k), jnp.float32)],
        in_specs=[mine, whole, whole, whole],
        out_specs=[whole, whole],
        compiler_params=params(16),
        cost_estimate=pl.CostEstimate(flops=6 * 2 * k * k * n, bytes_accessed=4 * k * n * 4, transcendentals=0),
        name="second_gram",
    )(partial, other, self_row, direction)


def first_state_kernel(alpha_ref, direction_ref, image_ref, out_ref):
    k, n = direction_ref.shape
    alpha = alpha_ref[:, :k]
    both = left_t(alpha, jnp.concatenate([direction_ref[...], image_ref[...]], axis=1))
    out_ref[:, :n] = both[:, :n]
    out_ref[:, n:] = direction_ref[...] - both[:, n:]


def first_state(alpha, direction, image):
    k, n = direction.shape
    whole = pl.BlockSpec(memory_space=pltpu.VMEM)
    return pl.pallas_call(
        first_state_kernel,
        out_shape=jax.ShapeDtypeStruct((k, 2 * n), jnp.float32),
        in_specs=[whole] * 3,
        out_specs=whole,
        compiler_params=params(16),
        cost_estimate=pl.CostEstimate(flops=6 * 2 * 2 * k * k * n, bytes_accessed=4 * k * n * 4, transcendentals=0),
        name="first_state",
    )(alpha, direction, image)


def last_update_kernel(*refs, count):
    part_refs = refs[:count]
    alpha_ref, state_ref, direction_ref, image_ref, charge_ref, out_ref = refs[count:]
    total = sum_of([ref[...] for ref in part_refs])
    k, n = direction_ref.shape
    gram = unfold(total)
    (alpha,) = eliminate([jnp.concatenate([0.5 * (gram + gram.T), alpha_ref[:, k:]], axis=1)])
    both = left_t(alpha, jnp.concatenate([direction_ref[...], image_ref[...]], axis=1))
    charge_ref[...] = state_ref[:, :n] + both[:, :n]
    out_ref[...] = state_ref[:, n:] - both[:, n:]


def last_update(parts, alpha, state, direction, image):
    k, n = direction.shape
    whole = pl.BlockSpec(memory_space=pltpu.VMEM)
    return pl.pallas_call(
        functools.partial(last_update_kernel, count=len(parts)),
        out_shape=[jax.ShapeDtypeStruct((k, n), jnp.float32)] * 2,
        in_specs=[whole] * (len(parts) + 4),
        out_specs=[whole] * 2,
        compiler_params=params(16),
        cost_estimate=pl.CostEstimate(flops=6 * 3 * 2 * k * k * n, bytes_accessed=4 * k * n * 6, transcendentals=0),
        name="last_update",
    )(*parts, alpha, state, direction, image)


def per_device_grouped(right_side, atom_centers, tessera_owner, tessera_angles, self_term):
    columns, shard = right_side.shape
    n_tgt = lax.axis_size("tgt")
    n_src = lax.axis_size("src")
    t = lax.axis_index("tgt")
    s = lax.axis_index("src")
    copies = n_tgt // GROUP
    member = t % GROUP
    ours = t // GROUP
    width = shard * n_src

    def swap(value, bits):
        return lax.ppermute(value, "tgt", [(i, i ^ bits) for i in range(n_tgt)])

    def swap_core(value):
        return lax.ppermute(value, "src", [(0, 1), (1, 0)])

    angles = lax.optimization_barrier(tessera_angles.reshape(2, -1, 128))
    offsets = lax.optimization_barrier(unit_offsets(angles)).reshape(3, -1)
    starts = [((member ^ bits) + GROUP * c) * width + s * shard for bits in range(GROUP) for c in range(copies)]
    starts += [(member + GROUP * c) * width + (1 - s) * shard for c in range(copies)]
    pos = chosen_positions(atom_centers, tessera_owner[None, :], offsets, jnp.stack(starts).astype(jnp.int32), shard)
    n_near = copies * shard
    n_all = GROUP * n_near
    target_pos = jnp.concatenate([pos[:, :n_near], pos[:, n_all:]], axis=1)
    kerns = entries(pos[:, :n_near], target_pos, 1)

    def beside(near, far):
        return jnp.where(ours == 0, jnp.concatenate([near, far], axis=1), jnp.concatenate([far, near], axis=1))

    self_near = self_term[None, :]
    right_far, self_far, kerns = lax.optimization_barrier((swap(right_side, GROUP), swap(self_near, GROUP), kerns))
    direction = beside(right_side, right_far)
    self_row = beside(self_near, self_far)
    charges = direction.astype(jnp.bfloat16)
    gathered = [charges] + [swap(charges, bits) for bits in range(1, GROUP)]
    kerns = [*kerns, *entries(pos[:, n_near:n_all], target_pos, GROUP - 1)]

    def group_sum_parts(value):
        value = value + swap_core(value)
        return [value] + [swap(value, bits) for bits in range(1, GROUP)]

    def mine(value):
        return lax.dynamic_slice_in_dim(value, ours * shard, shard, 1)

    to_other = apply_entries(gathered, kerns, first=n_near, m=n_near)
    other = swap_core(to_other)
    image, gram = first_gram(apply_entries(gathered, kerns, m=n_near), other, self_row, direction)
    alpha, later, charges = first_update(group_sum_parts(gram), image, direction)

    gathered = [swap(charges, bits) for bits in range(1, GROUP)]
    partial = apply_entries([charges], kerns[:1])
    for j in (2, 1, 0):
        partial = apply_entries([gathered[j]], [kerns[j + 1]], partial)
    state = first_state(alpha, right_side, mine(image))
    image, gram = second_gram(partial, swap_core(partial[:, n_near:]), self_row, later)
    return tuple(last_update(group_sum_parts(gram), alpha, state, mine(later), mine(image)))


def solution(mesh):
    n_tgt, n_src = mesh.shape["tgt"], mesh.shape["src"]

    def run(right_side, atom_centers, tessera_owner, tessera_angles, self_term):
        total = right_side.shape[1]
        stored = 2 * (total // n_src) * (total // GROUP)
        grouped = n_tgt == 2 * GROUP and n_src == 2 and stored <= STORED_LIMIT
        return jax.shard_map(
            per_device_grouped if grouped else per_device_general,
            mesh=mesh,
            in_specs=(P("conf", ("tgt", "src")), P("conf", None), P(), P(), P(("tgt", "src"))),
            out_specs=(P("conf", ("tgt", "src")), P("conf", ("tgt", "src"))),
            check_vma=False,
        )(right_side, atom_centers, tessera_owner, tessera_angles, self_term)

    return run
```

```python
import functools

import jax
import jax.numpy as jnp
from jax import lax
from jax.experimental import pallas as pl
from jax.experimental.pallas import tpu as pltpu
from jax.sharding import PartitionSpec as P

ITERS = 2
GROUP = 4
LOW = 256
FEATURES = 48
UNROLL = 10
BLOCK = 8
STORED_LIMIT = 32 * 2**20

soft_square = 0.09
probe_radius = 0.15
HIGHEST = lax.Precision.HIGHEST
MIB = 2**20


def params(mib, **kw):
    return pltpu.CompilerParams(vmem_limit_bytes=mib * MIB, **kw)


def positions(atom_centers, tessera_owner, tessera_angles):
    base = jnp.take(atom_centers, tessera_owner, axis=1)
    return base + probe_radius * unit_offsets(tessera_angles)


def unit_offsets(tessera_angles):
    azimuth = tessera_angles[0]
    polar = tessera_angles[1]
    sine = jnp.sin(polar)
    return jnp.stack([jnp.cos(azimuth) * sine, jnp.sin(azimuth) * sine, jnp.cos(polar)])


def tile_apply(total, source_pos, charges, target_pos):
    diff = source_pos[0][:, None] - target_pos[0][None, :]
    dist_sq = diff * diff
    diff = source_pos[1][:, None] - target_pos[1][None, :]
    dist_sq = dist_sq + diff * diff
    diff = source_pos[2][:, None] - target_pos[2][None, :]
    dist_sq = dist_sq + diff * diff
    kern = lax.rsqrt(dist_sq + soft_square).astype(jnp.bfloat16)
    return total + jnp.dot(charges, kern, preferred_element_type=jnp.float32)


def products(left, right):
    return lax.dot_general(
        left,
        right,
        (((1,), (1,)), ((), ())),
        precision=HIGHEST,
        preferred_element_type=jnp.float32,
    )


def chol_solve(matrix, rhs):
    lower = jnp.linalg.cholesky(matrix)
    middle = lax.linalg.triangular_solve(lower, rhs, left_side=True, lower=True)
    return lax.linalg.triangular_solve(lower, middle, left_side=True, lower=True, transpose_a=True)


def per_device_general(right_side, atom_centers, tessera_owner, tessera_angles, self_term):
    shard = right_side.shape[1]
    columns = right_side.shape[0]
    n_src = lax.axis_size("src")
    tgt_index = lax.axis_index("tgt")
    src_index = lax.axis_index("src")
    allpos = positions(atom_centers, tessera_owner, tessera_angles)

    def residual_norm(residual):
        return lax.psum(products(residual, residual), ("tgt", "src"))

    solution = jnp.zeros_like(right_side)
    residual = right_side
    direction = right_side
    norm_now = residual_norm(residual)
    for step in range(ITERS):
        charges = direction.astype(jnp.bfloat16)
        width = shard * n_src
        target_pos = lax.dynamic_slice_in_dim(allpos, tgt_index * width, width, 1)
        empty = jnp.zeros((columns, width), jnp.float32)
        piece = lax.all_gather(charges, "tgt", axis=1, tiled=True)
        sub = min(piece.shape[1], shard)
        count = piece.shape[1] // sub

        def one_block(j, acc):
            column = j * sub
            row_first = column // shard * width + src_index * shard + column % shard
            source_pos = lax.dynamic_slice_in_dim(allpos, row_first, sub, 1)
            part = lax.dynamic_slice_in_dim(piece, j * sub, sub, 1)
            return tile_apply(acc, source_pos, part, target_pos)

        partial_value = lax.fori_loop(0, count, one_block, empty)
        near = lax.psum_scatter(partial_value, "src", scatter_dimension=1, tiled=True)
        image = near + self_term[None, :] * direction
        gram = lax.psum(products(direction, image), ("tgt", "src"))
        alpha = chol_solve(gram, norm_now)
        solution = solution + jnp.dot(alpha.T, direction, precision=HIGHEST)
        residual = residual - jnp.dot(alpha.T, image, precision=HIGHEST)
        if step + 1 < ITERS:
            norm_next = residual_norm(residual)
            beta = chol_solve(norm_now, norm_next)
            direction = residual + jnp.dot(beta.T, direction, precision=HIGHEST)
            norm_now = norm_next
    return (solution, residual)


def three_parts(value):
    first = value.astype(jnp.bfloat16)
    rest = value - first.astype(jnp.float32)
    second = rest.astype(jnp.bfloat16)
    third = (rest - second.astype(jnp.float32)).astype(jnp.bfloat16)
    return first, second, third


def position_kernel(
    starts, table_hbm, owner_hbm, offset_ref, out_ref, table_ref, owner_ref, rows_ref, parts_ref, table_sem, owner_sem, *, chunk, count, rows
):
    table_copy = pltpu.make_async_copy(table_hbm, table_ref, table_sem)
    owner_copy = pltpu.make_async_copy(owner_hbm, owner_ref, owner_sem)
    table_copy.start()
    owner_copy.start()
    atoms = table_ref.shape[1]
    last = (atoms - 1) // LOW
    for axis in range(3):
        at = axis * rows + last
        rows_ref[at : (axis + 1) * rows, :] = jnp.zeros((rows - last, LOW), jnp.float32)
    table_copy.wait()
    owner_copy.wait()
    for row in range(last + 1):
        wide = min(LOW, atoms - row * LOW)
        values = table_ref[:, row * LOW : row * LOW + wide]
        for axis in range(3):
            at = axis * rows + row
            rows_ref[at : at + 1, :wide] = values[axis : axis + 1]
    for part, value in enumerate(three_parts(rows_ref[...])):
        parts_ref[:, part * LOW : (part + 1) * LOW] = value

    def one(j, carry):
        first = pl.multiple_of(starts[j], chunk)
        at = pl.multiple_of(j * chunk, chunk)
        owner = owner_ref[:, pl.ds(first, chunk)]
        low = lax.broadcasted_iota(jnp.int32, (LOW, chunk), 0) == (owner & (LOW - 1))
        low = low.astype(jnp.bfloat16)
        rows_of = jnp.dot(parts_ref[...], jnp.concatenate([low] * 3, axis=0), preferred_element_type=jnp.float32)
        high = lax.broadcasted_iota(jnp.int32, (rows, chunk), 0) == (owner // LOW)
        for axis in range(3):
            base = jnp.sum(jnp.where(high, rows_of[axis * rows : (axis + 1) * rows], 0.0), axis=0, keepdims=True)
            out_ref[axis : axis + 1, pl.ds(at, chunk)] = base + probe_radius * offset_ref[axis : axis + 1, pl.ds(first, chunk)]
        return carry

    lax.fori_loop(0, count, one, 0, unroll=UNROLL)


def in_hbm(array):
    return pltpu.with_memory_space_constraint(array, pltpu.HBM)


def chosen_positions(atom_centers, owner, offsets, starts, chunk):
    count = starts.shape[0]
    atoms = atom_centers.shape[1]
    rows = -(-atoms // (16 * LOW)) * 16
    whole = pl.BlockSpec(memory_space=pltpu.VMEM)
    far = pl.BlockSpec(memory_space=pltpu.HBM)
    return pl.pallas_call(
        functools.partial(position_kernel, chunk=chunk, count=count, rows=rows),
        out_shape=jax.ShapeDtypeStruct((3, count * chunk), jnp.float32),
        in_specs=[pl.BlockSpec(memory_space=pltpu.SMEM), far, far, whole],
        out_specs=whole,
        scratch_shapes=[
            pltpu.VMEM(atom_centers.shape, jnp.float32),
            pltpu.VMEM(owner.shape, jnp.int32),
            pltpu.VMEM((3 * rows, LOW), jnp.float32),
            pltpu.VMEM((3 * rows, 3 * LOW), jnp.bfloat16),
            pltpu.SemaphoreType.DMA,
            pltpu.SemaphoreType.DMA,
        ],
        compiler_params=params(24),
        cost_estimate=pl.CostEstimate(flops=2 * 9 * rows * LOW * count * chunk, bytes_accessed=4 * atoms * 3, transcendentals=0),
        name="positions",
    )(starts, in_hbm(atom_centers), in_hbm(owner), offsets)


def features(pos, source):
    first, second, third = three_parts(pos)
    x1, x2, x3 = (part.astype(jnp.float32) for part in (first, second, third))
    square_high, square_low, _ = three_parts(x1 * x1)
    rest = 2.0 * (x1 * x2) + (2.0 * (x1 * x3) + x2 * x2) + 2.0 * (x2 * x3)
    rest = rest[0:1] + rest[1:2] + rest[2:3]
    rest = list(three_parts(rest if source else rest + soft_square))
    one = jnp.ones_like(rest[0])
    ones = [one] * 9
    squares = [square_high, square_low, *rest]
    scale = -2.0 if source else 1.0
    parts = [(scale * part).astype(jnp.bfloat16) for part in (x1, x2, x3)]
    large, small = [], []
    for axis in range(3):
        c = slice(axis, axis + 1)
        mine = [square_high[c], square_low[c]]
        large += [parts[0][c], *(mine + [one, one] if source else [one, one] + mine)]
    for pair in [(0, 1), (1, 0), (1, 1), (0, 2), (2, 0), (1, 2), (2, 1), (2, 2)]:
        small.append(parts[pair[0] if source else pair[1]])
    small += rest + [one] * 3 if source else [one] * 3 + rest
    pad = [jnp.zeros_like(one)] * (FEATURES - 45)
    return jnp.concatenate(large + small + pad, axis=0)


def entry_kernel(source_ref, target_ref, *refs):
    out_refs, (source_rows, target_cols) = refs[:-2], refs[-2:]
    n = source_ref.shape[1]
    source_rows[...] = features(source_ref[...], True).T
    target_cols[...] = features(target_ref[...], False)
    n_out, m = out_refs[0].shape
    step, wide = min(n_out, 1024), min(m, 1024)
    for piece, out_ref in enumerate(out_refs):

        def one(i, carry, piece=piece, out_ref=out_ref):
            at = pl.multiple_of(i * step, step)
            rows = source_rows[pl.ds(piece * n_out + at, step), :]
            for j in range(0, m, wide):
                dist_sq = jnp.dot(rows, target_cols[:, j : j + wide], preferred_element_type=jnp.float32)
                out_ref[pl.ds(at, step), j : j + wide] = lax.rsqrt(dist_sq).astype(jnp.bfloat16)
            return carry

        lax.fori_loop(0, n_out // step, one, 0)


def entries(source_pos, target_pos, pieces):
    n, m = source_pos.shape[1], target_pos.shape[1]
    whole = pl.BlockSpec(memory_space=pltpu.VMEM)
    return pl.pallas_call(
        entry_kernel,
        out_shape=[jax.ShapeDtypeStruct((n // pieces, m), jnp.bfloat16)] * pieces,
        in_specs=[whole, whole],
        out_specs=[whole] * pieces,
        scratch_shapes=[pltpu.VMEM((n, FEATURES), jnp.bfloat16), pltpu.VMEM((FEATURES, m), jnp.bfloat16)],
        compiler_params=params(32),
        cost_estimate=pl.CostEstimate(flops=12 * n * m, bytes_accessed=2 * n * m, transcendentals=n * m),
        name="entries",
    )(source_pos, target_pos)


def apply_kernel(*refs, pieces, more, first):
    charge_refs, kern_refs, out_ref = refs[:pieces], refs[pieces : 2 * pieces], refs[-1]
    wide = 512
    for j in range(0, out_ref.shape[1], wide):
        total = refs[2 * pieces][:, j : j + wide] if more else None
        for charge_ref, kern_ref in zip(charge_refs, kern_refs):
            kern = kern_ref[:, first + j : first + j + wide]
            part = jnp.dot(charge_ref[...], kern, preferred_element_type=jnp.float32)
            total = part if total is None else total + part
        out_ref[:, j : j + wide] = total


def apply_entries(charges, kerns, total=None, first=0, m=None):
    pieces = len(charges)
    k, n = charges[0].shape
    m = kerns[0].shape[1] if m is None else m
    whole = pl.BlockSpec(memory_space=pltpu.VMEM)
    more = [] if total is None else [total]
    return pl.pallas_call(
        functools.partial(apply_kernel, pieces=pieces, more=bool(more), first=first),
        out_shape=jax.ShapeDtypeStruct((k, m), jnp.float32),
        in_specs=[whole] * (2 * pieces + len(more)),
        out_specs=whole,
        compiler_params=params(32),
        cost_estimate=pl.CostEstimate(flops=k * n, bytes_accessed=n, transcendentals=0),
        name="apply",
    )(*charges, *kerns, *more)


def dots(left, right):
    return lax.dot_general(left, right, (((1,), (1,)), ((), ())), precision=HIGHEST, preferred_element_type=jnp.float32)


def left_t(left, right):
    return lax.dot_general(left, right, (((0,), (0,)), ((), ())), precision=HIGHEST, preferred_element_type=jnp.float32)


def mul(left, right):
    return jnp.dot(left, right, precision=HIGHEST, preferred_element_type=jnp.float32)


def inverse_of_pair(a, b, c):
    scale = 1.0 / (a * c - b * b)
    return c * scale, -b * scale, a * scale


def eliminate_block(system, first, row_of):
    col = [jnp.broadcast_to(system[:, first + j : first + j + 1], system.shape) for j in range(BLOCK)]
    row = [system[first + j : first + j + 1, :] for j in range(BLOCK)]
    lower = {(r, c): col[c][first + r : first + r + 1] for c in range(BLOCK) for r in range(c, BLOCK)}

    def entry(r, c):
        return lower[max(r, c), min(r, c)]

    inverses = []
    for p in range(0, BLOCK, 2):
        a, b, d = inverse_of_pair(entry(p, p), entry(p + 1, p), entry(p + 1, p + 1))
        inverses.append((a, b, d))
        for r in range(BLOCK - 1, p + 1, -1):
            x, y = entry(r, p), entry(r, p + 1)
            f0, f1 = x * a + y * b, x * b + y * d
            for c in range(p + 2, r + 1):
                lower[r, c] = lower[r, c] - (f0 * entry(c, p) + f1 * entry(c, p + 1))
            row[r] = row[r] - (f0 * row[p] + f1 * row[p + 1])
    solved = [None] * BLOCK
    for p in range(BLOCK - 2, -1, -2):
        y0, y1 = row[p], row[p + 1]
        for c in range(p + 2, BLOCK):
            y0, y1 = y0 - entry(c, p) * solved[c], y1 - entry(c, p + 1) * solved[c]
        a, b, d = inverses[p // 2]
        solved[p], solved[p + 1] = a * y0 + b * y1, b * y0 + d * y1
    rest = system
    for j in range(0, BLOCK, 2):
        rest = rest - (col[j] * solved[j] + col[j + 1] * solved[j + 1])
    for j in range(BLOCK):
        rest = jnp.where(row_of == first + j, solved[j], rest)
    return rest


def eliminate(systems):
    k = systems[0].shape[0]
    row_of = lax.broadcasted_iota(jnp.int32, systems[0].shape, 0)
    for first in range(0, k, BLOCK):
        systems = [eliminate_block(system, first, row_of) for system in systems]
    return [system[:, k:] for system in systems]


def fold(square):
    half = square.shape[0] // 2
    return jnp.concatenate([square[:half], square[half:]], axis=1)


def unfold(folded):
    k = folded.shape[1] // 2
    return jnp.concatenate([folded[:, :k], folded[:, k:]], axis=0)


def first_gram_kernel(own_ref, other_ref, self_ref, direction_ref, image_ref, gram_ref):
    direction = direction_ref[...]
    image = own_ref[...] + other_ref[...] + self_ref[...] * direction
    image_ref[...] = image
    k = direction.shape[0]
    both = dots(jnp.concatenate([direction, image], axis=0), image)
    gram_ref[:k, :] = jnp.concatenate([both[:k], both[k:]], axis=1)
    gram_ref[k:, :] = fold(dots(direction, direction))


def first_gram(partial, other, self_row, direction):
    k, n = direction.shape
    whole = pl.BlockSpec(memory_space=pltpu.VMEM)
    return pl.pallas_call(
        first_gram_kernel,
        out_shape=[jax.ShapeDtypeStruct((k, n), jnp.float32), jax.ShapeDtypeStruct((k + k // 2, 2 * k), jnp.float32)],
        in_specs=[whole] * 4,
        out_specs=[whole, whole],
        compiler_params=params(8),
        cost_estimate=pl.CostEstimate(flops=6 * 2 * 3 * k * k * n, bytes_accessed=4 * k * n * 4, transcendentals=0),
        name="first_gram",
    )(partial, other, self_row, direction)


def first_update_kernel(*refs, count):
    part_refs, (image_ref, direction_ref, alpha_ref, next_ref, charges_ref) = refs[:count], refs[count:]
    total = sum_of([ref[...] for ref in part_refs])
    k = total.shape[1] // 2
    gram, image_sq, norm = total[:k, :k], total[:k, k:], unfold(total[k:, :])
    norm = 0.5 * (norm + norm.T)
    unit = (lax.broadcasted_iota(jnp.int32, (k, k), 0) == lax.broadcasted_iota(jnp.int32, (k, k), 1)).astype(jnp.float32)
    alpha, inverse = eliminate([
        jnp.concatenate([0.5 * (gram + gram.T), norm], axis=1),
        jnp.concatenate([norm, unit], axis=1),
    ])
    both = mul(jnp.concatenate([gram, image_sq], axis=0), alpha)
    cross = both[:k]
    norm_next = norm - cross - cross.T + left_t(alpha, both[k:])
    beta = mul(inverse, norm_next)
    alpha_ref[:, :k] = alpha
    alpha_ref[:, k:] = norm_next
    direction = direction_ref[...]
    weights = jnp.concatenate([beta, -alpha], axis=0)
    later = direction + left_t(weights, jnp.concatenate([direction, image_ref[...]], axis=0))
    next_ref[...] = later
    charges_ref[...] = later.astype(jnp.bfloat16)


def sum_of(values):
    while len(values) > 1:
        values = [values[i] + values[i + 1] for i in range(0, len(values), 2)]
    return values[0]


def first_update(parts, image, direction):
    k, n = direction.shape
    whole = pl.BlockSpec(memory_space=pltpu.VMEM)
    return pl.pallas_call(
        functools.partial(first_update_kernel, count=len(parts)),
        out_shape=[
            jax.ShapeDtypeStruct((k, 2 * k), jnp.float32),
            jax.ShapeDtypeStruct((k, n), jnp.float32),
            jax.ShapeDtypeStruct((k, n), jnp.bfloat16),
        ],
        in_specs=[whole] * (len(parts) + 2),
        out_specs=[whole] * 3,
        compiler_params=params(16),
        cost_estimate=pl.CostEstimate(flops=6 * 2 * 2 * k * k * n, bytes_accessed=4 * k * n * 5, transcendentals=0),
        name="first_update",
    )(*parts, image, direction)


def second_gram_kernel(own_ref, other_ref, self_ref, direction_ref, image_ref, gram_ref):
    direction = direction_ref[...]
    image = own_ref[...] + other_ref[...] + self_ref[...] * direction
    image_ref[...] = image
    k = direction.shape[0]
    gram_ref[...] = fold(dots(direction, image))


def second_gram(partial, other, self_row, direction):
    k, n = direction.shape
    mine = pl.BlockSpec((k, n), lambda i: (0, 0))
    whole = pl.BlockSpec(memory_space=pltpu.VMEM)
    return pl.pallas_call(
        second_gram_kernel,
        grid=(1,),
        out_shape=[jax.ShapeDtypeStruct((k, n), jnp.float32), jax.ShapeDtypeStruct((k // 2, 2 * k), jnp.float32)],
        in_specs=[mine, whole, whole, whole],
        out_specs=[whole, whole],
        compiler_params=params(16),
        cost_estimate=pl.CostEstimate(flops=6 * 2 * k * k * n, bytes_accessed=4 * k * n * 4, transcendentals=0),
        name="second_gram",
    )(partial, other, self_row, direction)


def first_state_kernel(alpha_ref, direction_ref, image_ref, out_ref):
    k, n = direction_ref.shape
    alpha = alpha_ref[:, :k]
    both = left_t(alpha, jnp.concatenate([direction_ref[...], image_ref[...]], axis=1))
    out_ref[:, :n] = both[:, :n]
    out_ref[:, n:] = direction_ref[...] - both[:, n:]


def first_state(alpha, direction, image):
    k, n = direction.shape
    whole = pl.BlockSpec(memory_space=pltpu.VMEM)
    return pl.pallas_call(
        first_state_kernel,
        out_shape=jax.ShapeDtypeStruct((k, 2 * n), jnp.float32),
        in_specs=[whole] * 3,
        out_specs=whole,
        compiler_params=params(16),
        cost_estimate=pl.CostEstimate(flops=6 * 2 * 2 * k * k * n, bytes_accessed=4 * k * n * 4, transcendentals=0),
        name="first_state",
    )(alpha, direction, image)


def last_update_kernel(*refs, count):
    part_refs = refs[:count]
    alpha_ref, state_ref, direction_ref, image_ref, charge_ref, out_ref = refs[count:]
    total = sum_of([ref[...] for ref in part_refs])
    k, n = direction_ref.shape
    gram = unfold(total)
    (alpha,) = eliminate([jnp.concatenate([0.5 * (gram + gram.T), alpha_ref[:, k:]], axis=1)])
    both = left_t(alpha, jnp.concatenate([direction_ref[...], image_ref[...]], axis=1))
    charge_ref[...] = state_ref[:, :n] + both[:, :n]
    out_ref[...] = state_ref[:, n:] - both[:, n:]


def last_update(parts, alpha, state, direction, image):
    k, n = direction.shape
    whole = pl.BlockSpec(memory_space=pltpu.VMEM)
    return pl.pallas_call(
        functools.partial(last_update_kernel, count=len(parts)),
        out_shape=[jax.ShapeDtypeStruct((k, n), jnp.float32)] * 2,
        in_specs=[whole] * (len(parts) + 4),
        out_specs=[whole] * 2,
        compiler_params=params(16),
        cost_estimate=pl.CostEstimate(flops=6 * 3 * 2 * k * k * n, bytes_accessed=4 * k * n * 6, transcendentals=0),
        name="last_update",
    )(*parts, alpha, state, direction, image)


def per_device_grouped(right_side, atom_centers, tessera_owner, tessera_angles, self_term):
    columns, shard = right_side.shape
    n_tgt = lax.axis_size("tgt")
    n_src = lax.axis_size("src")
    t = lax.axis_index("tgt")
    s = lax.axis_index("src")
    copies = n_tgt // GROUP
    member = t % GROUP
    ours = t // GROUP
    width = shard * n_src

    def swap(value, bits):
        return lax.ppermute(value, "tgt", [(i, i ^ bits) for i in range(n_tgt)])

    def swap_core(value):
        return lax.ppermute(value, "src", [(0, 1), (1, 0)])

    angles = lax.optimization_barrier(tessera_angles.reshape(2, -1, 128))
    offsets = lax.optimization_barrier(unit_offsets(angles)).reshape(3, -1)
    starts = [((member ^ bits) + GROUP * c) * width + s * shard for bits in range(GROUP) for c in range(copies)]
    starts += [(member + GROUP * c) * width + (1 - s) * shard for c in range(copies)]
    pos = chosen_positions(atom_centers, tessera_owner[None, :], offsets, jnp.stack(starts).astype(jnp.int32), shard)
    n_near = copies * shard
    n_all = GROUP * n_near
    target_pos = jnp.concatenate([pos[:, :n_near], pos[:, n_all:]], axis=1)
    kerns = entries(pos[:, :n_near], target_pos, 1)

    def beside(near, far):
        return jnp.where(ours == 0, jnp.concatenate([near, far], axis=1), jnp.concatenate([far, near], axis=1))

    self_near = self_term[None, :]
    right_far, self_far, kerns = lax.optimization_barrier((swap(right_side, GROUP), swap(self_near, GROUP), kerns))
    direction = beside(right_side, right_far)
    self_row = beside(self_near, self_far)
    charges = direction.astype(jnp.bfloat16)
    gathered = [charges] + [swap(charges, bits) for bits in range(1, GROUP)]
    kerns = [*kerns, *entries(pos[:, n_near:n_all], target_pos, GROUP - 1)]

    def group_sum_parts(value):
        value = value + swap_core(value)
        return [value] + [swap(value, bits) for bits in range(1, GROUP)]

    def mine(value):
        return lax.dynamic_slice_in_dim(value, ours * shard, shard, 1)

    to_other = apply_entries(gathered, kerns, first=n_near, m=n_near)
    other = swap_core(to_other)
    image, gram = first_gram(apply_entries(gathered, kerns, m=n_near), other, self_row, direction)
    alpha, later, charges = first_update(group_sum_parts(gram), image, direction)

    gathered = [swap(charges, bits) for bits in range(1, GROUP)]
    partial = apply_entries([charges], kerns[:1])
    for j in (2, 1, 0):
        partial = apply_entries([gathered[j]], [kerns[j + 1]], partial)
    state = first_state(alpha, right_side, mine(image))
    image, gram = second_gram(partial, swap_core(partial[:, n_near:]), self_row, later)
    return tuple(last_update(group_sum_parts(gram), alpha, state, mine(later), mine(image)))


def solution(mesh):
    n_tgt, n_src = mesh.shape["tgt"], mesh.shape["src"]

    def run(right_side, atom_centers, tessera_owner, tessera_angles, self_term):
        total = right_side.shape[1]
        stored = 2 * (total // n_src) * (total // GROUP)
        grouped = n_tgt == 2 * GROUP and n_src == 2 and stored <= STORED_LIMIT
        return jax.shard_map(
            per_device_grouped if grouped else per_device_general,
            mesh=mesh,
            in_specs=(P("conf", ("tgt", "src")), P("conf", None), P(), P(), P(("tgt", "src"))),
            out_specs=(P("conf", ("tgt", "src")), P("conf", ("tgt", "src"))),
            check_vma=False,
        )(right_side, atom_centers, tessera_owner, tessera_angles, self_term)

    return run
```
